32 devices in a mesh: groups: 2 (over x), ctx: 16 (over z, y, core).
Axes of the slice: x: 2, y: 2, z: 4, core: 2. Of those that a mesh axis runs over, the one named last changes fastest.
Arguments:
- queries: bfloat16 [2048, 64, 576], P(('groups', 'ctx')), parts along dimension 0, may hold values from -26 to 26
- latent_cache: bfloat16 [8192, 576], P(('groups', 'ctx')), parts along dimension 0, may hold values from -6 to 6
- tile_lists: int32 [32, 32], P(('groups', 'ctx')), parts along dimension 0, may hold values from -1 to 63, as said below
Outputs:
- attended: bfloat16 [2048, 64, 512], P(('groups', 'ctx')), parts along dimension 0
The draws below stay inside these ranges and needn't reach their ends.
There are 2 independent parts, one for each index of `groups`. The reference program is written for one: setup_inputs(seed, part) draws one part's arguments, and reference() takes and returns one part's arrays. A program takes and returns all parts, laid end to end along the dimension named above; each array names one. Nothing has to cross between parts.
Inputs may be any that keep to these rules, and one draw needn't show every extreme that they name: `tile_lists`: each row names distinct tiles that end at or before the block's own last tile 4 * b + 3, which is always named; no row names more than 1 tiles held by one device, and exactly 1 of the block's own device; valid entries come first, then -1; row b has min(32, 1 * (b + 1)) valid entries.
All inputs are finite; a program needn't handle non-finite values.
Results may differ from the reference program's by a relative error of at most 0.0034.
Values may be sent and summed in bfloat16 or wider, within the bound.
No kernel may reach another device: no remote copies, remote signals or barrier semaphores. Data moves between devices by JAX's collectives and lax.ppermute only.
A program may use at most 128 MiB of HBM per device.

```python
import jax
import jax.numpy as jnp
from jax import lax

H = 64
LAT = 512
ROPE = 64
TILE = 64
TOPK = 32
CAP = 1
TILES_DEV = 4
Q_DEV = 64
C_DEV = 256
CTX = 4096
NTILES = 64
N_CTX = 16


def draw_latent_cache(key, part):
    key = jax.random.fold_in(key, 5)
    shape = (CTX, LAT + ROPE)
    base = jnp.clip(jax.random.normal(key, shape, jnp.float32), -6.0, 6.0)
    return base.astype(jnp.bfloat16)


def draw_queries(key, part):
    key = jax.random.fold_in(key, 7)
    first = jax.random.fold_in(key, 0)
    shape = (N_CTX * Q_DEV, H, LAT + ROPE)
    base = jnp.clip(jax.random.normal(first, shape, jnp.float32), -6.0, 6.0)
    return base.astype(jnp.bfloat16)


def draw_tile_lists(key, part):
    key = jax.random.fold_in(key, 11)
    count = NTILES
    block = jnp.arange(N_CTX, dtype=jnp.int32)[:, None]
    tile = jnp.arange(count, dtype=jnp.int32)[None, :]
    holder = tile // TILES_DEV
    noise = jax.random.randint(key, (N_CTX, count), 0, 32768)
    last = block * TILES_DEV + TILES_DEV - 1
    causal = tile <= last
    level = jnp.where(tile == last, 6, jnp.where(tile == last - 1, 5, jnp.where(tile == 0, 4, 0)))
    recent = jnp.where(holder >= block - 3, 16384, 0)
    score = (level * 65536 + noise + recent) * count + tile
    grouped = score.reshape(N_CTX, N_CTX, TILES_DEV)
    rank = jnp.sum((grouped[:, :, None, :] > grouped[:, :, :, None]).astype(jnp.int32), axis=-1)
    keep = causal & (rank.reshape(N_CTX, count) < CAP)
    masked = jnp.where(keep, score, -1)
    values, picked = lax.top_k(masked, TOPK)
    return jnp.where(values >= 0, picked, -1).astype(jnp.int32)


def setup_inputs(seed: int = 0, part: int = 0) -> dict:
    key_of = jax.random.split(jax.random.key(seed), 4)
    part_splits = jax.random.split(jax.random.fold_in(key_of[3], part), 4)
    return {
        "queries": draw_queries(jax.random.fold_in(jax.random.fold_in(key_of[3], part), 71), part),
        "latent_cache": draw_latent_cache(jax.random.fold_in(jax.random.fold_in(key_of[3], part), 71), part),
        "tile_lists": draw_tile_lists(jax.random.fold_in(jax.random.fold_in(key_of[3], part), 71), part),
    }


softmax_scale = 192.0 ** -0.5


def attend(query_rows, keys, key_pos, key_ok, query_pos):
    scores = jnp.einsum("qhc,kc->qhk", query_rows.astype(jnp.float32), keys.astype(jnp.float32)) * softmax_scale
    allowed = key_ok[None, :] & (key_pos[None, :] <= query_pos[:, None])
    allowed = allowed[:, None, :]
    scores = jnp.where(allowed, scores, -1e30)
    top = jnp.max(scores, axis=-1, keepdims=True)
    expo = jnp.where(allowed, jnp.exp(scores - top), 0.0)
    total = jnp.sum(expo, axis=-1, keepdims=True)
    weights = lax.optimization_barrier(expo.astype(jnp.bfloat16))
    values = keys[:, :LAT].astype(jnp.float32)
    summed = jnp.einsum("qhk,kc->qhc", weights.astype(jnp.float32), values)
    return (summed / total).astype(jnp.bfloat16)


def reference(queries, latent_cache, tile_lists):
    width = LAT + ROPE
    tiles = latent_cache.reshape(NTILES, TILE, width)
    blocks = queries.reshape(N_CTX, Q_DEV, H, width)
    offsets = jnp.arange(TILE, dtype=jnp.int32)

    def one_block(operands):
        query_rows, listing, index = operands
        safe = jnp.clip(listing, 0, NTILES - 1).astype(jnp.int32)
        keys = jnp.take(tiles, safe, axis=0).reshape(TOPK * TILE, width)
        key_pos = (safe[:, None] * TILE + offsets[None, :]).reshape(-1)
        key_ok = jnp.repeat(listing >= 0, TILE)
        query_pos = index * C_DEV + C_DEV - Q_DEV + jnp.arange(Q_DEV, dtype=jnp.int32)
        return attend(query_rows, keys, key_pos, key_ok, query_pos)

    result = lax.map(one_block, (blocks, tile_lists, jnp.arange(N_CTX, dtype=jnp.int32)))
    return result.reshape(N_CTX * Q_DEV, H, LAT)
```

```python
import functools
import math

import jax
import jax.numpy as jnp
from jax import lax
from jax.experimental import pallas as pl
from jax.experimental.pallas import tpu as pltpu
from jax.sharding import PartitionSpec as P

LAT = 512
TILE = 64
TOPK = 32
CAP = 1
TILES_DEV = 4
ROW = 4


softmax_scale = 192.0 ** (-0.5)
LOG2E_SCALE = softmax_scale * math.log2(math.e)
MASKED = -1e30


def slot_ranks(holders):
    same = (holders[:, None] == holders[None, :]) & (holders[:, None] >= 0)
    count = holders.shape[0]
    earlier = (
        jnp.arange(count, dtype=jnp.int32)[:, None] < jnp.arange(count, dtype=jnp.int32)[None, :]
    )
    return jnp.sum((same & earlier).astype(jnp.int32), axis=0)


def slot_table(match, ranks, local_tile):
    slots = jnp.arange(CAP, dtype=jnp.int32)
    hits = match[..., None] & (ranks[..., None] == slots)
    return jnp.sum(jnp.where(hits, local_tile[..., None] + 1, 0), axis=-2) - 1


def shards_general(queries, latent_cache, tile_lists):
    width = latent_cache.shape[1]
    listing = tile_lists[0]
    me = lax.axis_index("ctx")
    valid = listing >= 0
    flat_cache = latent_cache.reshape(TILES_DEV, TILE * width)
    peers = lax.axis_size("ctx")
    holders = jnp.where(valid, listing // TILES_DEV, -1)
    ranks = slot_ranks(holders)
    lists_all = lax.all_gather(tile_lists, "ctx", axis=0, tiled=True)
    holders_all = jnp.where(lists_all >= 0, lists_all // TILES_DEV, -1)
    ranks_all = jax.vmap(slot_ranks)(holders_all)
    wanted = slot_table(holders_all == me, ranks_all, lists_all % TILES_DEV)
    outgoing = jnp.take(flat_cache, jnp.clip(wanted, 0, TILES_DEV - 1), axis=0)
    outgoing = jnp.where((wanted >= 0)[..., None], outgoing, jnp.zeros_like(outgoing))
    incoming = lax.all_to_all(outgoing, "ctx", split_axis=0, concat_axis=0, tiled=True)
    incoming = incoming.reshape(peers * CAP, TILE * width)
    position = jnp.clip(holders, 0, peers - 1) * CAP + jnp.clip(ranks, 0, CAP - 1)
    keys = jnp.take(incoming, position, axis=0)
    keys = keys.reshape(TOPK * TILE, width)
    safe = jnp.clip(listing, 0, None)
    offsets = jnp.arange(TILE, dtype=jnp.int32)
    key_pos = (safe[:, None] * TILE + offsets[None, :]).reshape(-1)
    key_ok = jnp.repeat(valid, TILE)
    q_count = queries.shape[0]
    context_dev = TILES_DEV * TILE
    query_pos = me * context_dev + context_dev - q_count + jnp.arange(q_count, dtype=jnp.int32)
    scores = (
        jnp.einsum("qhc,kc->qhk", queries, keys, preferred_element_type=jnp.float32) * softmax_scale
    )
    allowed = (key_ok[None, :] & (key_pos[None, :] <= query_pos[:, None]))[:, None, :]
    scores = jnp.where(allowed, scores, MASKED)
    top = jnp.max(scores, axis=-1, keepdims=True)
    expo = jnp.where(allowed, jnp.exp(scores - top), 0.0)
    total = jnp.sum(expo, axis=-1, keepdims=True)
    weights = expo.astype(jnp.bfloat16)
    summed = jnp.einsum("qhk,kc->qhc", weights, keys[:, :LAT], preferred_element_type=jnp.float32)
    return (summed / total).astype(jnp.bfloat16)


def pick_kernel(outs_of, sel_ref, *refs):
    n_src = 1 + max(src for parts in outs_of for src, _ in parts)
    sources, outs, sems = refs[:n_src], refs[n_src : n_src + len(outs_of)], refs[-1]
    copies = []
    for out, parts in zip(outs, outs_of):
        for at, (src, entry) in enumerate(parts):
            tile = pl.multiple_of(sel_ref[entry] * TILE, TILE)
            copies.append(
                pltpu.make_async_copy(
                    sources[src].at[pl.ds(tile, TILE), :],
                    out.at[pl.ds(at * TILE, TILE), :],
                    sems.at[len(copies)],
                )
            )
    for copy in copies:
        copy.start()
    for copy in copies:
        copy.wait()


def pick_tiles(sel, sources, outs_of):
    width = sources[0].shape[1]
    total = sum(len(parts) for parts in outs_of)
    return pl.pallas_call(
        functools.partial(pick_kernel, outs_of),
        in_specs=[pl.BlockSpec(memory_space=pltpu.SMEM)]
        + [pl.BlockSpec(memory_space=pl.ANY)] * len(sources),
        out_specs=[pl.BlockSpec(memory_space=pl.ANY)] * len(outs_of),
        out_shape=[
            jax.ShapeDtypeStruct((len(parts) * TILE, width), sources[0].dtype) for parts in outs_of
        ],
        scratch_shapes=[pltpu.SemaphoreType.DMA((total,))],
        cost_estimate=pl.CostEstimate(
            flops=0, transcendentals=0, bytes_accessed=4 * total * TILE * width
        ),
        name="pick_tiles",
    )(sel, *sources)


def attend_kernel(heads, parts, sel_ref, bias_ref, q_ref, *refs):
    n_src = 1 + max(src for src, _, _ in parts)
    sources, (out_ref, keys_ref, sems) = refs[:n_src], refs[n_src:]

    @pl.when(pl.program_id(0) == 0)
    def _():
        copies = []
        for at, (src, entry, tile) in enumerate(parts):
            row = tile * TILE if entry is None else pl.multiple_of(sel_ref[entry] * TILE, TILE)
            copies.append(
                pltpu.make_async_copy(
                    sources[src].at[pl.ds(row, TILE), :],
                    keys_ref.at[pl.ds(at * TILE, TILE), :],
                    sems.at[at],
                )
            )
        for copy in copies:
            copy.start()
        for copy in copies:
            copy.wait()

    rows = q_ref.shape[0]
    count = keys_ref.shape[0]
    scores = lax.dot_general(
        q_ref[...], keys_ref[...], (((1,), (1,)), ((), ())), preferred_element_type=jnp.float32
    )
    scores = scores.reshape(rows // heads, heads, count) + bias_ref[...][:, None, :]
    scores = scores.reshape(rows, count)
    top = jnp.max(scores, axis=1, keepdims=True)
    expo = jnp.exp2(scores * LOG2E_SCALE - top * LOG2E_SCALE)
    total = jnp.sum(expo, axis=1, keepdims=True)
    summed = jnp.dot(
        expo.astype(jnp.bfloat16), keys_ref[:, :LAT], preferred_element_type=jnp.float32
    )
    out_ref[...] = (summed * (1.0 / total)).astype(out_ref.dtype)


def attend(queries, bias, sel, sources, parts):
    count, heads, width = queries.shape
    keys = len(parts) * TILE
    step = 16
    rows = step * heads
    out = pl.pallas_call(
        functools.partial(attend_kernel, heads, parts),
        grid=(count // step,),
        in_specs=[
            pl.BlockSpec(memory_space=pltpu.SMEM),
            pl.BlockSpec((step, keys), lambda i: (i, 0)),
            pl.BlockSpec((rows, width), lambda i: (i, 0)),
        ]
        + [pl.BlockSpec(memory_space=pl.ANY)] * len(sources),
        out_specs=pl.BlockSpec((rows, LAT), lambda i: (i, 0)),
        out_shape=jax.ShapeDtypeStruct((count * heads, LAT), jnp.bfloat16),
        scratch_shapes=[
            pltpu.VMEM((keys, width), jnp.bfloat16),
            pltpu.SemaphoreType.DMA((len(parts),)),
        ],
        compiler_params=pltpu.CompilerParams(
            vmem_limit_bytes=48 << 20, dimension_semantics=("arbitrary",)
        ),
        cost_estimate=pl.CostEstimate(
            flops=2 * count * heads * keys * (width + LAT),
            transcendentals=count * heads * keys,
            bytes_accessed=2 * count * heads * (width + LAT),
        ),
        name="attend",
    )(sel, bias, queries.reshape(count * heads, width), *sources)
    return out.reshape(count, heads, LAT)


def shards_rows(queries, latent_cache, tile_lists):
    size = lax.axis_size("ctx")
    depth = size // ROW
    me = lax.axis_index("ctx")
    z, r = me // ROW, me % ROW
    up = [(i, i + ROW) for i in range(size - ROW)]
    down = [(i + ROW, i) for i in range(size - ROW)]
    beside = {m: [(i, i ^ m) for i in range(size)] for m in range(1, ROW)}

    above = [latent_cache]
    if depth > 1:
        above.append(lax.ppermute(latent_cache, "ctx", up))
    lists = jnp.concatenate(
        [tile_lists] + [lax.ppermute(tile_lists, "ctx", beside[m]) for m in range(1, ROW)]
    )
    below = lax.ppermute(lists, "ctx", down)

    def local_tile(listing, holder):
        hit = (listing >= 0) & (listing // TILES_DEV == holder)
        return jnp.sum(jnp.where(hit, listing % TILES_DEV, 0), axis=1)

    wanted = [local_tile(lists, me - ROW * k) for k in range(depth)]
    sources, parts = [], {}

    first = range(min(2, depth - 1) if depth > 1 else 1)
    sel = jnp.concatenate([wanted[k] for k in first])
    sent = pick_tiles(
        sel, [above[k] for k in first], [[(k, k * ROW + m) for k in first] for m in range(1, ROW)]
    )
    for m in range(1, ROW):
        for k in first:
            parts[k, m] = (len(sources), None, k)
        sources.append(lax.ppermute(sent[m - 1], "ctx", beside[m]))
    for k in range(2, depth - 1):
        above.append(lax.ppermute(above[k - 1], "ctx", up))
        sent = pick_tiles(wanted[k], [above[k]], [[(0, m)] for m in range(1, ROW)])
        for m in range(1, ROW):
            parts[k, m] = (len(sources), None, 0)
            sources.append(lax.ppermute(sent[m - 1], "ctx", beside[m]))
    if depth > 1:
        last = depth - 1
        sel = local_tile(below, me - ROW * (last - 1))
        sent = pick_tiles(sel, [above[last - 1]], [[(0, m)] for m in range(ROW)])
        for m in range(ROW):
            parts[last, m] = (len(sources), None, 0)
            hop = [(i, (i + ROW) ^ m) for i in range(ROW * (last - 1), ROW * last)]
            sources.append(lax.ppermute(sent[m], "ctx", hop))
    for k in range(max(1, depth - 1)):
        parts[k, 0] = (len(sources), k, 0)
        sources.append(above[k])
    order = [(k, m) for k in range(depth) for m in range(ROW)]
    own = jnp.stack([wanted[k][0] for k in range(max(1, depth - 1))])

    slot = jnp.arange(len(order) * TILE, dtype=jnp.int32)
    k, m, offset = slot // (ROW * TILE), slot // TILE % ROW, slot % TILE
    seen = jnp.where(k == 0, (r ^ m) <= r, k <= z)
    query = jnp.arange(queries.shape[0], dtype=jnp.int32)[:, None]
    seen = seen & ((k > 0) | (m > 0) | (offset <= query))
    bias = jnp.where(seen, 0.0, MASKED).astype(jnp.float32)
    return attend(queries, bias, own, sources, [parts[key] for key in order])


def solution(mesh):
    placed = (
        P(("groups", "ctx"), None, None),
        P(("groups", "ctx"), None),
        P(("groups", "ctx"), None),
    )
    size = mesh.shape["ctx"]
    shards = shards_rows if size <= TOPK and size % ROW == 0 else shards_general
    return jax.shard_map(
        shards,
        mesh=mesh,
        in_specs=placed,
        out_specs=P(("groups", "ctx"), None, None),
        check_vma=False,
    )
```

```python
import functools
import math

import jax
import jax.numpy as jnp
from jax import lax
from jax.experimental import pallas as pl
from jax.experimental.pallas import tpu as pltpu
from jax.sharding import PartitionSpec as P

LAT = 512
TILE = 64
TOPK = 32
CAP = 1
TILES_DEV = 4
ROW = 4
DEPTH = 4


softmax_scale = 192.0 ** (-0.5)
LOG2E_SCALE = softmax_scale * math.log2(math.e)
MASKED = -1e30


def slot_ranks(holders):
    same = (holders[:, None] == holders[None, :]) & (holders[:, None] >= 0)
    count = holders.shape[0]
    earlier = (
        jnp.arange(count, dtype=jnp.int32)[:, None] < jnp.arange(count, dtype=jnp.int32)[None, :]
    )
    return jnp.sum((same & earlier).astype(jnp.int32), axis=0)


def slot_table(match, ranks, local_tile):
    slots = jnp.arange(CAP, dtype=jnp.int32)
    hits = match[..., None] & (ranks[..., None] == slots)
    return jnp.sum(jnp.where(hits, local_tile[..., None] + 1, 0), axis=-2) - 1


def shards_general(queries, latent_cache, tile_lists):
    width = latent_cache.shape[1]
    listing = tile_lists[0]
    me = lax.axis_index("ctx")
    valid = listing >= 0
    flat_cache = latent_cache.reshape(TILES_DEV, TILE * width)
    peers = lax.axis_size("ctx")
    holders = jnp.where(valid, listing // TILES_DEV, -1)
    ranks = slot_ranks(holders)
    lists_all = lax.all_gather(tile_lists, "ctx", axis=0, tiled=True)
    holders_all = jnp.where(lists_all >= 0, lists_all // TILES_DEV, -1)
    ranks_all = jax.vmap(slot_ranks)(holders_all)
    wanted = slot_table(holders_all == me, ranks_all, lists_all % TILES_DEV)
    outgoing = jnp.take(flat_cache, jnp.clip(wanted, 0, TILES_DEV - 1), axis=0)
    outgoing = jnp.where((wanted >= 0)[..., None], outgoing, jnp.zeros_like(outgoing))
    incoming = lax.all_to_all(outgoing, "ctx", split_axis=0, concat_axis=0, tiled=True)
    incoming = incoming.reshape(peers * CAP, TILE * width)
    position = jnp.clip(holders, 0, peers - 1) * CAP + jnp.clip(ranks, 0, CAP - 1)
    keys = jnp.take(incoming, position, axis=0)
    keys = keys.reshape(TOPK * TILE, width)
    safe = jnp.clip(listing, 0, None)
    offsets = jnp.arange(TILE, dtype=jnp.int32)
    key_pos = (safe[:, None] * TILE + offsets[None, :]).reshape(-1)
    key_ok = jnp.repeat(valid, TILE)
    q_count = queries.shape[0]
    context_dev = TILES_DEV * TILE
    query_pos = me * context_dev + context_dev - q_count + jnp.arange(q_count, dtype=jnp.int32)
    scores = (
        jnp.einsum("qhc,kc->qhk", queries, keys, preferred_element_type=jnp.float32) * softmax_scale
    )
    allowed = (key_ok[None, :] & (key_pos[None, :] <= query_pos[:, None]))[:, None, :]
    scores = jnp.where(allowed, scores, MASKED)
    top = jnp.max(scores, axis=-1, keepdims=True)
    expo = jnp.where(allowed, jnp.exp(scores - top), 0.0)
    total = jnp.sum(expo, axis=-1, keepdims=True)
    weights = expo.astype(jnp.bfloat16)
    summed = jnp.einsum("qhk,kc->qhc", weights, keys[:, :LAT], preferred_element_type=jnp.float32)
    return (summed / total).astype(jnp.bfloat16)


def side_by_side(sel_ref, entry, blocks, out_ref):
    for at in range(0, len(blocks), 2):
        pair = []
        for upper in (False, True):
            block = blocks[at + upper][...]
            swapped = jnp.concatenate([block[:, TILE:], block[:, :TILE]], axis=1)
            odd = sel_ref[entry + at + upper] % 2 == 1
            pair.append(jnp.where(odd != upper, swapped, block))
        out_ref[:, at * TILE : (at + 2) * TILE] = jnp.concatenate(
            [pair[0][:, :TILE], pair[1][:, TILE:]], axis=1
        )


def tile_blocks(width, entries):
    return [
        pl.BlockSpec((width, 2 * TILE), lambda i, sel, entry=entry: (0, sel[entry] // 2))
        for entry in entries
    ]


def pick_kernel(sel_ref, *refs):
    side_by_side(sel_ref, 0, refs[:-1], refs[-1])


def pick_tiles(sel, caches):
    width = caches[0].shape[0]
    columns = len(caches) * TILE
    return pl.pallas_call(
        pick_kernel,
        grid_spec=pltpu.PrefetchScalarGridSpec(
            num_scalar_prefetch=1,
            grid=(1,),
            in_specs=tile_blocks(width, range(len(caches))),
            out_specs=pl.BlockSpec((width, columns), lambda i, sel: (0, 0)),
        ),
        out_shape=jax.ShapeDtypeStruct((width, columns), caches[0].dtype),
        compiler_params=pltpu.CompilerParams(vmem_limit_bytes=6 << 20),
        cost_estimate=pl.CostEstimate(
            flops=0, transcendentals=0, bytes_accessed=4 * columns * width
        ),
        name="pick_tiles",
    )(sel, *caches)


def attend_kernel(heads, entry, first, sel_ref, *refs):
    count = ROW if not first else 2 * ROW
    blocks, refs = refs[:count], refs[count:]
    if first:
        bias_ref, q_ref, out_ref, top_ref, total_ref, keys_ref = refs
    else:
        far_ref, q_ref, mean_ref, top_ref, total_ref, out_ref, keys_ref = refs
    rows = q_ref.shape[0]
    lanes = 2 * TILE
    z = lax.axis_index("ctx") // ROW

    def pieces(array):
        return [array[:, at : at + lanes] for at in range(0, array.shape[1], lanes)]

    def load():
        side_by_side(sel_ref, entry, blocks, keys_ref)
        if not first:
            keys_ref[:, count * TILE :] = far_ref[...]

    def merge():
        scores = jnp.dot(q_ref[...], keys_ref[...], preferred_element_type=jnp.float32)
        if first:
            scores = scores.reshape(rows // heads, heads, -1) + bias_ref[...][:, None, :]
            scores = pieces(scores.reshape(rows, -1))
        else:
            scores = pieces(scores)
            far_bias = jnp.where(z >= DEPTH - 1, 0.0, MASKED)
            half = len(scores) // 2
            scores[half:] = [piece + far_bias for piece in scores[half:]]
        top = jnp.max(functools.reduce(jnp.maximum, scores), axis=1, keepdims=True)
        top = jnp.broadcast_to(top, (rows, lanes))
        if not first:
            top_before = top_ref[...]
            top = jnp.maximum(top, top_before)
        scaled_top = top * LOG2E_SCALE
        expo = [jnp.exp2(piece * LOG2E_SCALE - scaled_top) for piece in scores]
        total = jnp.sum(functools.reduce(jnp.add, expo), axis=1, keepdims=True)
        total = jnp.broadcast_to(total, (rows, lanes))
        expo = jnp.concatenate([piece.astype(jnp.bfloat16) for piece in expo], axis=1)
        summed = lax.dot_general(
            expo, keys_ref[:LAT, :], (((1,), (1,)), ((), ())), preferred_element_type=jnp.float32
        )
        summed = pieces(summed)
        if first:
            scale = 1.0 / total
            result = [piece * scale for piece in summed]
            top_ref[...] = top
            total_ref[...] = total
        else:
            before = total_ref[...] * jnp.exp2(top_before * LOG2E_SCALE - scaled_top)
            scale = 1.0 / (total + before)
            share = before * scale
            result = [
                piece * scale + mean.astype(jnp.float32) * share
                for piece, mean in zip(summed, pieces(mean_ref[...]))
            ]
        for at, piece in enumerate(result):
            out_ref[:, at * lanes : (at + 1) * lanes] = piece.astype(out_ref.dtype)

    if first:
        pl.when(pl.program_id(0) == 0)(load)
        merge()
    else:
        seen = z >= DEPTH - 2
        pl.when(seen & (pl.program_id(0) == 0))(load)
        pl.when(seen)(merge)

        @pl.when(jnp.logical_not(seen))
        def _():
            out_ref[...] = mean_ref[...]


def attend(queries, sel, entry, caches, bias=None, far=None, state=()):
    count, heads, width = queries.shape
    first = bias is not None
    keys = 2 * ROW * TILE
    step = 16
    rows = step * heads

    def rows_of(width):
        return pl.BlockSpec((rows, width), lambda i, sel: (i, 0))

    mean = jax.ShapeDtypeStruct((count * heads, LAT), jnp.bfloat16)
    stats = jax.ShapeDtypeStruct((count * heads, 2 * TILE), jnp.float32)
    grid_spec = pltpu.PrefetchScalarGridSpec(
        num_scalar_prefetch=1,
        grid=(count // step,),
        in_specs=tile_blocks(width, range(entry, entry + len(caches)))
        + [
            pl.BlockSpec((step, keys), lambda i, sel: (i, 0))
            if first
            else pl.BlockSpec(far.shape, lambda i, sel: (0, 0))
        ]
        + [rows_of(width)]
        + ([] if first else [rows_of(LAT), rows_of(2 * TILE), rows_of(2 * TILE)]),
        out_specs=[rows_of(LAT), rows_of(2 * TILE), rows_of(2 * TILE)] if first else rows_of(LAT),
        scratch_shapes=[pltpu.VMEM((width, keys), jnp.bfloat16)],
    )
    return pl.pallas_call(
        functools.partial(attend_kernel, heads, entry, first),
        grid_spec=grid_spec,
        out_shape=[mean, stats, stats] if first else mean,
        compiler_params=pltpu.CompilerParams(
            vmem_limit_bytes=24 << 20, dimension_semantics=("arbitrary",)
        ),
        cost_estimate=pl.CostEstimate(
            flops=2 * count * heads * keys * (width + LAT),
            transcendentals=count * heads * keys,
            bytes_accessed=2 * count * heads * (width + LAT),
        ),
        name="attend_near" if first else "attend_rest",
    )(sel, *caches, bias if first else far, queries.reshape(count * heads, width), *state)


def shards_rows(queries, latent_cache, tile_lists):
    size = lax.axis_size("ctx")
    span = size - ROW
    me = lax.axis_index("ctx")
    z, r = me // ROW, me % ROW

    def beside(array, m):
        return lax.ppermute(array, "ctx", [(i, i ^ m) for i in range(size)])

    def further(array, rows, sources):
        return lax.ppermute(array, "ctx", [(i, i + ROW * rows) for i in sources])

    def named_tiles(listing, holders):
        hit = (listing >= 0) & (listing // TILES_DEV == holders[:, None])
        return jnp.sum(jnp.where(hit, listing % TILES_DEV, 0), axis=1)

    cache = latent_cache.T
    cache1 = further(cache, 1, range(span))
    far_list = lax.ppermute(tile_lists, "ctx", [(i + span, i) for i in range(ROW)])
    across = beside(cache, 2)
    row0 = [cache, beside(cache, 1), across, beside(across, 1)]

    slot = jnp.arange((DEPTH - 1) * ROW, dtype=jnp.int32)
    sel = named_tiles(tile_lists, ROW * (z - slot // ROW) + (r ^ slot % ROW))

    cache2 = further(cache1, 1, range(ROW, span))
    far = pick_tiles(named_tiles(far_list, me ^ jnp.arange(ROW, dtype=jnp.int32)), row0)
    far = further(far, DEPTH - 1, range(ROW))
    across = beside(cache1, 2)
    row1 = [cache1, beside(cache1, 1), across, beside(across, 1)]

    slot = jnp.arange(2 * ROW * TILE, dtype=jnp.int32)
    k, m, offset = slot // (ROW * TILE), slot // TILE % ROW, slot % TILE
    seen = jnp.where(k == 0, (r ^ m) <= r, k <= z)
    query = jnp.arange(queries.shape[0], dtype=jnp.int32)[:, None]
    seen = seen & ((k > 0) | (m > 0) | (offset <= query))
    bias = jnp.where(seen, 0.0, MASKED).astype(jnp.float32)

    state = attend(queries, sel, 0, [*row0, *row1], bias=bias)
    across, beside2 = beside(cache2, 2), beside(cache2, 1)
    across, *state = lax.optimization_barrier((across, *state))
    row2 = [cache2, beside2, across, beside(across, 1)]
    out = attend(queries, sel, 2 * ROW, row2, far=far, state=state)
    return out.reshape(*queries.shape[:2], LAT)


def solution(mesh):
    placed = (
        P(("groups", "ctx"), None, None),
        P(("groups", "ctx"), None),
        P(("groups", "ctx"), None),
    )
    size = mesh.shape["ctx"]
    shards = shards_rows if size == ROW * DEPTH else shards_general
    return jax.shard_map(
        shards,
        mesh=mesh,
        in_specs=placed,
        out_specs=P(("groups", "ctx"), None, None),
        check_vma=False,
    )
```

```python
import functools
import math

import jax
import jax.numpy as jnp
from jax import lax
from jax.experimental import pallas as pl
from jax.experimental.pallas import tpu as pltpu
from jax.sharding import PartitionSpec as P

LAT = 512
TILE = 64
TOPK = 32
CAP = 1
TILES_DEV = 4
ROW = 4
STAGES = 4
DEPTH = 4


softmax_scale = 192.0 ** (-0.5)
LOG2E_SCALE = softmax_scale * math.log2(math.e)
MASKED = -1e30


def slot_ranks(holders):
    same = (holders[:, None] == holders[None, :]) & (holders[:, None] >= 0)
    count = holders.shape[0]
    earlier = (
        jnp.arange(count, dtype=jnp.int32)[:, None] < jnp.arange(count, dtype=jnp.int32)[None, :]
    )
    return jnp.sum((same & earlier).astype(jnp.int32), axis=0)


def slot_table(match, ranks, local_tile):
    slots = jnp.arange(CAP, dtype=jnp.int32)
    hits = match[..., None] & (ranks[..., None] == slots)
    return jnp.sum(jnp.where(hits, local_tile[..., None] + 1, 0), axis=-2) - 1


def shards_general(queries, latent_cache, tile_lists):
    width = latent_cache.shape[1]
    listing = tile_lists[0]
    me = lax.axis_index("ctx")
    valid = listing >= 0
    flat_cache = latent_cache.reshape(TILES_DEV, TILE * width)
    peers = lax.axis_size("ctx")
    holders = jnp.where(valid, listing // TILES_DEV, -1)
    ranks = slot_ranks(holders)
    lists_all = lax.all_gather(tile_lists, "ctx", axis=0, tiled=True)
    holders_all = jnp.where(lists_all >= 0, lists_all // TILES_DEV, -1)
    ranks_all = jax.vmap(slot_ranks)(holders_all)
    wanted = slot_table(holders_all == me, ranks_all, lists_all % TILES_DEV)
    outgoing = jnp.take(flat_cache, jnp.clip(wanted, 0, TILES_DEV - 1), axis=0)
    outgoing = jnp.where((wanted >= 0)[..., None], outgoing, jnp.zeros_like(outgoing))
    incoming = lax.all_to_all(outgoing, "ctx", split_axis=0, concat_axis=0, tiled=True)
    incoming = incoming.reshape(peers * CAP, TILE * width)
    position = jnp.clip(holders, 0, peers - 1) * CAP + jnp.clip(ranks, 0, CAP - 1)
    keys = jnp.take(incoming, position, axis=0)
    keys = keys.reshape(TOPK * TILE, width)
    safe = jnp.clip(listing, 0, None)
    offsets = jnp.arange(TILE, dtype=jnp.int32)
    key_pos = (safe[:, None] * TILE + offsets[None, :]).reshape(-1)
    key_ok = jnp.repeat(valid, TILE)
    q_count = queries.shape[0]
    context_dev = TILES_DEV * TILE
    query_pos = me * context_dev + context_dev - q_count + jnp.arange(q_count, dtype=jnp.int32)
    scores = (
        jnp.einsum("qhc,kc->qhk", queries, keys, preferred_element_type=jnp.float32) * softmax_scale
    )
    allowed = (key_ok[None, :] & (key_pos[None, :] <= query_pos[:, None]))[:, None, :]
    scores = jnp.where(allowed, scores, MASKED)
    top = jnp.max(scores, axis=-1, keepdims=True)
    expo = jnp.where(allowed, jnp.exp(scores - top), 0.0)
    total = jnp.sum(expo, axis=-1, keepdims=True)
    weights = expo.astype(jnp.bfloat16)
    summed = jnp.einsum("qhk,kc->qhc", weights, keys[:, :LAT], preferred_element_type=jnp.float32)
    return (summed / total).astype(jnp.bfloat16)


def side_by_side(sel_ref, entry, blocks, out_ref):
    for at in range(0, len(blocks), 2):
        pair = []
        for upper in (False, True):
            block = blocks[at + upper][...]
            swapped = jnp.concatenate([block[:, TILE:], block[:, :TILE]], axis=1)
            odd = sel_ref[entry + at + upper] % 2 == 1
            pair.append(jnp.where(odd != upper, swapped, block))
        out_ref[:, at * TILE : (at + 2) * TILE] = jnp.concatenate(
            [pair[0][:, :TILE], pair[1][:, TILE:]], axis=1
        )


def tile_blocks(width, entries):
    return [
        pl.BlockSpec((width, 2 * TILE), lambda i, sel, entry=entry: (0, sel[entry] // 2))
        for entry in entries
    ]


def pick_kernel(sel_ref, *refs):
    side_by_side(sel_ref, 0, refs[:-1], refs[-1])


def pick_tiles(sel, caches):
    width = caches[0].shape[0]
    columns = len(caches) * TILE
    return pl.pallas_call(
        pick_kernel,
        grid_spec=pltpu.PrefetchScalarGridSpec(
            num_scalar_prefetch=1,
            grid=(1,),
            in_specs=tile_blocks(width, range(len(caches))),
            out_specs=pl.BlockSpec((width, columns), lambda i, sel: (0, 0)),
        ),
        out_shape=jax.ShapeDtypeStruct((width, columns), caches[0].dtype),
        compiler_params=pltpu.CompilerParams(vmem_limit_bytes=6 << 20),
        cost_estimate=pl.CostEstimate(
            flops=0, transcendentals=0, bytes_accessed=4 * columns * width
        ),
        name="pick_tiles",
    )(sel, *caches)


def stage_kernel(*refs):
    *refs, sems = refs
    half = len(refs) // 2
    copies = []
    for source_ref, out_ref in zip(refs[:half], refs[half:]):
        rows = source_ref.shape[0] // STAGES
        for at in range(STAGES):
            block = pl.ds(at * rows, rows)
            copies.append(
                pltpu.make_async_copy(
                    source_ref.at[block, :], out_ref.at[block, :], sems.at[len(copies)]
                )
            )
    for copy in copies:
        copy.start()
    for copy in copies:
        copy.wait()


def stage(*arrays):
    return pl.pallas_call(
        stage_kernel,
        in_specs=[pl.BlockSpec(memory_space=pltpu.HBM)] * len(arrays),
        out_specs=[pl.BlockSpec(memory_space=pltpu.VMEM)] * len(arrays),
        out_shape=[pltpu.VMEM(array.shape, array.dtype) for array in arrays],
        scratch_shapes=[pltpu.SemaphoreType.DMA((STAGES * len(arrays),))],
        compiler_params=pltpu.CompilerParams(vmem_limit_bytes=8 << 20),
        cost_estimate=pl.CostEstimate(
            flops=0, transcendentals=0, bytes_accessed=4 * sum(array.size for array in arrays)
        ),
        name="stage",
    )(*(pltpu.with_memory_space_constraint(array, pltpu.HBM) for array in arrays))


def attend_kernel(heads, step, first, sel_ref, *refs):
    count = 2 * ROW if first else ROW
    blocks, refs = refs[:count], refs[count:]
    if first:
        bias_ref, q_ref, out_ref, top_ref, total_ref, keys_ref = refs
    else:
        far_ref, q_ref, mean_ref, top_ref, total_ref, out_ref, keys_ref = refs
    rows = step
    lanes = 2 * TILE
    block = pl.ds(pl.multiple_of(pl.program_id(0) * rows, rows), rows)
    written = block if first else slice(None)
    z = lax.axis_index("ctx") // ROW

    def pieces(array):
        return [array[:, at : at + lanes] for at in range(0, array.shape[1], lanes)]

    def load():
        side_by_side(sel_ref, 0 if first else 2 * ROW, blocks, keys_ref)
        if not first:
            keys_ref[:, ROW * TILE :] = far_ref[...]

    def merge():
        scores = jnp.dot(q_ref[block, :], keys_ref[...], preferred_element_type=jnp.float32)
        if first:
            scores = scores.reshape(rows // heads, heads, -1) + bias_ref[...][:, None, :]
            scores = pieces(scores.reshape(rows, -1))
        else:
            scores = pieces(scores)
            far_bias = jnp.where(z >= DEPTH - 1, 0.0, MASKED)
            half = len(scores) // 2
            scores[half:] = [piece + far_bias for piece in scores[half:]]
        top = jnp.max(functools.reduce(jnp.maximum, scores), axis=1, keepdims=True)
        top = jnp.broadcast_to(top, (rows, lanes))
        if not first:
            top_before = top_ref[block, :]
            top = jnp.maximum(top, top_before)
        scaled_top = top * LOG2E_SCALE
        expo = [jnp.exp2(piece * LOG2E_SCALE - scaled_top) for piece in scores]
        total = jnp.sum(functools.reduce(jnp.add, expo), axis=1, keepdims=True)
        total = jnp.broadcast_to(total, (rows, lanes))
        expo = jnp.concatenate([piece.astype(jnp.bfloat16) for piece in expo], axis=1)
        summed = lax.dot_general(
            expo, keys_ref[:LAT, :], (((1,), (1,)), ((), ())), preferred_element_type=jnp.float32
        )
        summed = pieces(summed)
        if first:
            scale = 1.0 / total
            result = [piece * scale for piece in summed]
            top_ref[block, :] = top
            total_ref[block, :] = total
        else:
            before = total_ref[block, :] * jnp.exp2(top_before * LOG2E_SCALE - scaled_top)
            scale = 1.0 / (total + before)
            share = before * scale
            result = [
                piece * scale + mean.astype(jnp.float32) * share
                for piece, mean in zip(summed, pieces(mean_ref[block, :]))
            ]
        for at, piece in enumerate(result):
            out_ref[written, at * lanes : (at + 1) * lanes] = piece.astype(out_ref.dtype)

    if first:
        pl.when(pl.program_id(0) == 0)(load)
        merge()
    else:
        seen = z >= DEPTH - 2
        pl.when(seen & (pl.program_id(0) == 0))(load)
        pl.when(seen)(merge)

        @pl.when(jnp.logical_not(seen))
        def _():
            out_ref[...] = mean_ref[block, :]


def attend(queries, heads, sel, tiles, bias=None, state=()):
    count, width = queries.shape[0] // heads, queries.shape[1]
    first = bias is not None
    keys = 2 * ROW * TILE
    step = 16
    rows = step * heads

    def rows_of(width):
        return pl.BlockSpec((rows, width), lambda i, sel: (i, 0))

    if first:
        in_specs = tile_blocks(width, range(2 * ROW))
        in_specs.append(pl.BlockSpec((step, keys), lambda i, sel: (i, 0)))
        tiles = (*tiles, bias)
    else:
        in_specs = tile_blocks(width, range(2 * ROW, 3 * ROW))
        in_specs.append(pl.BlockSpec(memory_space=pltpu.VMEM))
    in_specs.append(pl.BlockSpec(memory_space=pltpu.VMEM))
    state_specs = [pl.BlockSpec(memory_space=pltpu.VMEM)] * 3
    shape, dtype = (count * heads, LAT), queries.dtype
    stats = pltpu.VMEM((count * heads, 2 * TILE), jnp.float32)
    grid_spec = pltpu.PrefetchScalarGridSpec(
        num_scalar_prefetch=1,
        grid=(count // step,),
        in_specs=in_specs if first else in_specs + state_specs,
        out_specs=state_specs if first else rows_of(LAT),
        scratch_shapes=[pltpu.VMEM((width, keys), jnp.bfloat16)],
    )
    return pl.pallas_call(
        functools.partial(attend_kernel, heads, rows, first),
        grid_spec=grid_spec,
        out_shape=[pltpu.VMEM(shape, dtype), stats, stats] if first else jax.ShapeDtypeStruct(shape, dtype),
        compiler_params=pltpu.CompilerParams(
            vmem_limit_bytes=24 << 20, dimension_semantics=("arbitrary",)
        ),
        cost_estimate=pl.CostEstimate(
            flops=2 * count * heads * keys * (width + LAT),
            transcendentals=count * heads * keys,
            bytes_accessed=2 * count * heads * (width + LAT),
        ),
        name="attend_near" if first else "attend_rest",
    )(sel, *tiles, queries, *state)


def shards_rows(queries, latent_cache, tile_lists):
    size = lax.axis_size("ctx")
    span = size - ROW
    me = lax.axis_index("ctx")
    z, r = me // ROW, me % ROW

    def beside(array, m):
        return lax.ppermute(array, "ctx", [(i, i ^ m) for i in range(size)])

    def further(array, rows, sources):
        return lax.ppermute(array, "ctx", [(i, i + ROW * rows) for i in sources])

    def named_tiles(listing, holders):
        hit = (listing >= 0) & (listing // TILES_DEV == holders[:, None])
        return jnp.sum(jnp.where(hit, listing % TILES_DEV, 0), axis=1)

    shape = queries.shape
    cache = latent_cache.T
    cache1 = further(cache, 1, range(span))
    across = beside(cache, 2)
    far_list = lax.ppermute(tile_lists, "ctx", [(i + span, i) for i in range(ROW)])
    queries, cache = stage(queries.reshape(-1, shape[2]), cache)
    cache, across = lax.optimization_barrier((cache, across))
    row0 = [cache, beside(cache, 1), across, beside(across, 1)]
    cache1, queries = lax.optimization_barrier((cache1, queries))

    slot = jnp.arange((DEPTH - 1) * ROW, dtype=jnp.int32)
    sel = named_tiles(tile_lists, ROW * (z - slot // ROW) + (r ^ slot % ROW))

    far = pick_tiles(named_tiles(far_list, me ^ jnp.arange(ROW, dtype=jnp.int32)), row0)
    cache2 = further(cache1, 1, range(ROW, span))
    across, beside1 = beside(cache1, 2), beside(cache1, 1)
    across, far = lax.optimization_barrier((across, far))
    far = further(far, DEPTH - 1, range(ROW))
    row1 = [cache1, beside1, across, beside(across, 1)]

    slot = jnp.arange(2 * ROW * TILE, dtype=jnp.int32)
    k, m, offset = slot // (ROW * TILE), slot // TILE % ROW, slot % TILE
    seen = jnp.where(k == 0, (r ^ m) <= r, k <= z)
    query = jnp.arange(shape[0], dtype=jnp.int32)[:, None]
    seen = seen & ((k > 0) | (m > 0) | (offset <= query))
    bias = jnp.where(seen, 0.0, MASKED).astype(jnp.float32)

    *row1, cache2 = lax.optimization_barrier((*row1, cache2))
    across, beside2 = beside(cache2, 2), beside(cache2, 1)
    state = attend(queries, shape[1], sel, [*row0, *row1], bias=bias)
    across, *state = lax.optimization_barrier((across, *state))
    row2 = [cache2, beside2, across, beside(across, 1)]
    out = attend(queries, shape[1], sel, [*row2, far], state=state)
    return out.reshape(*shape[:2], LAT)


def solution(mesh):
    placed = (
        P(("groups", "ctx"), None, None),
        P(("groups", "ctx"), None),
        P(("groups", "ctx"), None),
    )
    size = mesh.shape["ctx"]
    shards = shards_rows if size == ROW * DEPTH else shards_general
    return jax.shard_map(
        shards,
        mesh=mesh,
        in_specs=placed,
        out_specs=P(("groups", "ctx"), None, None),
        check_vma=False,
    )
```

```python
import functools
import math

import jax
import jax.numpy as jnp
from jax import lax
from jax.experimental import pallas as pl
from jax.experimental.pallas import tpu as pltpu
from jax.sharding import PartitionSpec as P

LAT = 512
TILE = 64
TOPK = 32
CAP = 1
TILES_DEV = 4
ROW = 4
STAGES = 4
BLOCKS = 4
DEPTH = 4


softmax_scale = 192.0 ** (-0.5)
LOG2E_SCALE = softmax_scale * math.log2(math.e)
MASKED = -1e30


def slot_ranks(holders):
    same = (holders[:, None] == holders[None, :]) & (holders[:, None] >= 0)
    count = holders.shape[0]
    earlier = (
        jnp.arange(count, dtype=jnp.int32)[:, None] < jnp.arange(count, dtype=jnp.int32)[None, :]
    )
    return jnp.sum((same & earlier).astype(jnp.int32), axis=0)


def slot_table(match, ranks, local_tile):
    slots = jnp.arange(CAP, dtype=jnp.int32)
    hits = match[..., None] & (ranks[..., None] == slots)
    return jnp.sum(jnp.where(hits, local_tile[..., None] + 1, 0), axis=-2) - 1


def shards_general(queries, latent_cache, tile_lists):
    width = latent_cache.shape[1]
    listing = tile_lists[0]
    me = lax.axis_index("ctx")
    valid = listing >= 0
    flat_cache = latent_cache.reshape(TILES_DEV, TILE * width)
    peers = lax.axis_size("ctx")
    holders = jnp.where(valid, listing // TILES_DEV, -1)
    ranks = slot_ranks(holders)
    lists_all = lax.all_gather(tile_lists, "ctx", axis=0, tiled=True)
    holders_all = jnp.where(lists_all >= 0, lists_all // TILES_DEV, -1)
    ranks_all = jax.vmap(slot_ranks)(holders_all)
    wanted = slot_table(holders_all == me, ranks_all, lists_all % TILES_DEV)
    outgoing = jnp.take(flat_cache, jnp.clip(wanted, 0, TILES_DEV - 1), axis=0)
    outgoing = jnp.where((wanted >= 0)[..., None], outgoing, jnp.zeros_like(outgoing))
    incoming = lax.all_to_all(outgoing, "ctx", split_axis=0, concat_axis=0, tiled=True)
    incoming = incoming.reshape(peers * CAP, TILE * width)
    position = jnp.clip(holders, 0, peers - 1) * CAP + jnp.clip(ranks, 0, CAP - 1)
    keys = jnp.take(incoming, position, axis=0)
    keys = keys.reshape(TOPK * TILE, width)
    safe = jnp.clip(listing, 0, None)
    offsets = jnp.arange(TILE, dtype=jnp.int32)
    key_pos = (safe[:, None] * TILE + offsets[None, :]).reshape(-1)
    key_ok = jnp.repeat(valid, TILE)
    q_count = queries.shape[0]
    context_dev = TILES_DEV * TILE
    query_pos = me * context_dev + context_dev - q_count + jnp.arange(q_count, dtype=jnp.int32)
    scores = (
        jnp.einsum("qhc,kc->qhk", queries, keys, preferred_element_type=jnp.float32) * softmax_scale
    )
    allowed = (key_ok[None, :] & (key_pos[None, :] <= query_pos[:, None]))[:, None, :]
    scores = jnp.where(allowed, scores, MASKED)
    top = jnp.max(scores, axis=-1, keepdims=True)
    expo = jnp.where(allowed, jnp.exp(scores - top), 0.0)
    total = jnp.sum(expo, axis=-1, keepdims=True)
    weights = expo.astype(jnp.bfloat16)
    summed = jnp.einsum("qhk,kc->qhc", weights, keys[:, :LAT], preferred_element_type=jnp.float32)
    return (summed / total).astype(jnp.bfloat16)


def side_by_side(sel_ref, entry, caches, out_ref):
    for at in range(0, len(caches), 2):
        pair = []
        for upper in (False, True):
            tile = sel_ref[entry + at + upper]
            start = pl.multiple_of(tile // 2 * 2 * TILE, 2 * TILE)
            block = caches[at + upper][:, pl.ds(start, 2 * TILE)]
            swapped = jnp.concatenate([block[:, TILE:], block[:, :TILE]], axis=1)
            pair.append(jnp.where((tile % 2 == 1) != upper, swapped, block))
        out_ref[:, at * TILE : (at + 2) * TILE] = jnp.concatenate(
            [pair[0][:, :TILE], pair[1][:, TILE:]], axis=1
        )


def pick_kernel(sel_ref, own_ref, *refs):
    *caches, sent_ref, kept_ref = refs
    side_by_side(sel_ref, 0, caches, sent_ref)
    side_by_side(own_ref, 0, caches, kept_ref)


def pick_tiles(sel, own, caches):
    width = caches[0].shape[0]
    columns = len(caches) * TILE
    vmem = pl.BlockSpec(memory_space=pltpu.VMEM)
    return pl.pallas_call(
        pick_kernel,
        in_specs=[pl.BlockSpec(memory_space=pltpu.SMEM)] * 2 + [vmem] * len(caches),
        out_specs=[vmem] * 2,
        out_shape=[jax.ShapeDtypeStruct((width, columns), caches[0].dtype)] * 2,
        compiler_params=pltpu.CompilerParams(vmem_limit_bytes=6 << 20),
        cost_estimate=pl.CostEstimate(
            flops=0, transcendentals=0, bytes_accessed=8 * columns * width
        ),
        name="pick_tiles",
    )(sel, own, *caches)


def pieces(array):
    return [array[:, at : at + 2 * TILE] for at in range(0, array.shape[1], 2 * TILE)]


def score(queries, keys):
    return jnp.dot(queries, keys, preferred_element_type=jnp.float32)


def weigh(scores, top):
    scaled_top = top * LOG2E_SCALE
    expo = [jnp.exp2(piece * LOG2E_SCALE - scaled_top) for piece in scores]
    total = jnp.sum(functools.reduce(jnp.add, expo), axis=1, keepdims=True)
    expo = jnp.concatenate([piece.astype(jnp.bfloat16) for piece in expo], axis=1)
    return expo, jnp.broadcast_to(total, top.shape)


def tops(scores):
    top = jnp.max(functools.reduce(jnp.maximum, scores), axis=1, keepdims=True)
    return jnp.broadcast_to(top, (top.shape[0], 2 * TILE))


def mix(expo, keys_ref):
    summed = lax.dot_general(
        expo, keys_ref[:LAT, :], (((1,), (1,)), ((), ())), preferred_element_type=jnp.float32
    )
    return pieces(summed)


def near_kernel(heads, sel_ref, *refs):
    caches, refs = refs[:ROW], refs[ROW:]
    own_ref, bias_ref, q_ref, mean_ref, top_ref, total_ref, keys_ref = refs
    half = ROW * TILE
    side_by_side(sel_ref, ROW, caches, keys_ref)
    keys_ref[:, half:] = own_ref[...]
    hidden = jnp.where(lax.axis_index("ctx") >= ROW, 0.0, MASKED)
    rows = q_ref.shape[0] // BLOCKS
    for at in range(BLOCKS):
        block = pl.ds(at * rows, rows)
        own = score(q_ref[block, :], own_ref[...])
        bias = bias_ref[pl.ds(at * (rows // heads), rows // heads), :]
        own = own.reshape(rows // heads, heads, -1) + bias[:, None, :]
        scores = [piece + hidden for piece in pieces(score(q_ref[block, :], keys_ref[:, :half]))]
        scores += pieces(own.reshape(rows, -1))
        top = tops(scores)
        expo, total = weigh(scores, top)
        scale = 1.0 / total
        for lane, piece in enumerate(mix(expo, keys_ref)):
            lanes = slice(lane * 2 * TILE, (lane + 1) * 2 * TILE)
            mean_ref[block, lanes] = (piece * scale).astype(mean_ref.dtype)
        top_ref[block, :] = top
        total_ref[block, :] = total


def rest_kernel(sel_ref, *refs):
    caches, refs = refs[:ROW], refs[ROW:]
    far_ref, q_ref, mean_ref, top_ref, total_ref, out_hbm, keys_ref, out_ref, sems = refs
    z = lax.axis_index("ctx") // ROW
    rows = q_ref.shape[0] // BLOCKS

    def put(at):
        block = pl.ds(at * rows, rows)
        return pltpu.make_async_copy(out_ref.at[block, :], out_hbm.at[block, :], sems.at[at])

    @pl.when(z >= DEPTH - 2)
    def _():
        half = ROW * TILE
        side_by_side(sel_ref, 2 * ROW, caches, keys_ref)
        keys_ref[:, half:] = far_ref[...]
        hidden = jnp.where(z >= DEPTH - 1, 0.0, MASKED)
        for at in range(BLOCKS):
            block = pl.ds(at * rows, rows)
            far = [piece + hidden for piece in pieces(score(q_ref[block, :], far_ref[...]))]
            scores = pieces(score(q_ref[block, :], keys_ref[:, :half])) + far
            top_before = top_ref[block, :]
            top = jnp.maximum(tops(scores), top_before)
            expo, total = weigh(scores, top)
            before = total_ref[block, :] * jnp.exp2((top_before - top) * LOG2E_SCALE)
            scale = 1.0 / (total + before)
            share = before * scale
            for lane, piece in enumerate(mix(expo, keys_ref)):
                lanes = slice(lane * 2 * TILE, (lane + 1) * 2 * TILE)
                mean = mean_ref[block, lanes].astype(jnp.float32)
                out_ref[block, lanes] = (piece * scale + mean * share).astype(out_ref.dtype)
            put(at).start()

    @pl.when(z < DEPTH - 2)
    def _():
        for at in range(BLOCKS):
            block = pl.ds(at * rows, rows)
            out_ref[block, :] = mean_ref[block, :]
            put(at).start()

    for at in range(BLOCKS):
        put(at).wait()


def attend(kernel, queries, sel, tiles, state=()):
    count, width = queries.shape
    keys = 2 * ROW * TILE
    vmem = pl.BlockSpec(memory_space=pltpu.VMEM)
    near = not state
    scratch = [pltpu.VMEM((width, keys), queries.dtype)]
    if near:
        stats = pltpu.VMEM((count, 2 * TILE), jnp.float32)
        out_shape = [pltpu.VMEM((count, LAT), queries.dtype), stats, stats]
    else:
        out_shape = jax.ShapeDtypeStruct((count, LAT), queries.dtype)
        scratch += [pltpu.VMEM((count, LAT), queries.dtype), pltpu.SemaphoreType.DMA((BLOCKS,))]
    return pl.pallas_call(
        kernel,
        in_specs=[pl.BlockSpec(memory_space=pltpu.SMEM)] + [vmem] * (len(tiles) + 1 + len(state)),
        out_specs=[vmem] * 3 if near else pl.BlockSpec(memory_space=pl.ANY),
        out_shape=out_shape,
        scratch_shapes=scratch,
        compiler_params=pltpu.CompilerParams(vmem_limit_bytes=24 << 20),
        cost_estimate=pl.CostEstimate(
            flops=2 * count * keys * (width + LAT),
            transcendentals=count * keys,
            bytes_accessed=2 * count * (width + LAT),
        ),
        name="attend_near" if near else "attend_rest",
    )(sel, *tiles, queries, *state)


def stage_kernel(*refs):
    *refs, sems = refs
    half = len(refs) // 2
    copies = []
    for source_ref, out_ref in zip(refs[:half], refs[half:]):
        rows = source_ref.shape[0] // STAGES
        for at in range(STAGES):
            block = pl.ds(at * rows, rows)
            copies.append(
                pltpu.make_async_copy(
                    source_ref.at[block, :], out_ref.at[block, :], sems.at[len(copies)]
                )
            )
    for copy in copies:
        copy.start()
    for copy in copies:
        copy.wait()


def stage(*arrays):
    return pl.pallas_call(
        stage_kernel,
        in_specs=[pl.BlockSpec(memory_space=pltpu.HBM)] * len(arrays),
        out_specs=[pl.BlockSpec(memory_space=pltpu.VMEM)] * len(arrays),
        out_shape=[pltpu.VMEM(array.shape, array.dtype) for array in arrays],
        scratch_shapes=[pltpu.SemaphoreType.DMA((STAGES * len(arrays),))],
        compiler_params=pltpu.CompilerParams(vmem_limit_bytes=8 << 20),
        cost_estimate=pl.CostEstimate(
            flops=0, transcendentals=0, bytes_accessed=4 * sum(array.size for array in arrays)
        ),
        name="stage",
    )(*(pltpu.with_memory_space_constraint(array, pltpu.HBM) for array in arrays))


def shards_rows(queries, latent_cache, tile_lists):
    size = lax.axis_size("ctx")
    span = size - ROW
    me = lax.axis_index("ctx")
    z, r = me // ROW, me % ROW

    def beside(array, m):
        return lax.ppermute(array, "ctx", [(i, i ^ m) for i in range(size)])

    def further(array, rows, sources):
        return lax.ppermute(array, "ctx", [(i, i + ROW * rows) for i in sources])

    def named_tiles(listing, holders):
        hit = (listing >= 0) & (listing // TILES_DEV == holders[:, None])
        return jnp.sum(jnp.where(hit, listing % TILES_DEV, 0), axis=1)

    shape = queries.shape
    cache = latent_cache.T
    cache1 = further(cache, 1, range(span))
    across = beside(cache, 2)
    far_list = lax.ppermute(tile_lists, "ctx", [(i + span, i) for i in range(ROW)])
    (cache,) = stage(cache)
    cache, across = lax.optimization_barrier((cache, across))
    row0 = [cache, beside(cache, 1), across, beside(across, 1)]

    slot = jnp.arange((DEPTH - 1) * ROW, dtype=jnp.int32)
    sel = named_tiles(tile_lists, ROW * (z - slot // ROW) + (r ^ slot % ROW))

    far_sel = named_tiles(far_list, me ^ jnp.arange(ROW, dtype=jnp.int32))
    far, keys0 = pick_tiles(far_sel, sel, row0)
    cache2 = further(cache1, 1, range(ROW, span))
    across = beside(cache1, 2)
    queries = queries.reshape(-1, shape[2])
    far, queries = lax.optimization_barrier((far, queries))
    (queries,) = stage(queries)
    cache1, queries = lax.optimization_barrier((cache1, queries))
    beside1 = beside(cache1, 1)
    across, far, queries = lax.optimization_barrier((across, far, queries))
    far = further(far, DEPTH - 1, range(ROW))
    row1 = [cache1, beside1, across, beside(across, 1)]

    slot = jnp.arange(ROW * TILE, dtype=jnp.int32)
    m, offset = slot // TILE, slot % TILE
    query = jnp.arange(shape[0], dtype=jnp.int32)[:, None]
    seen = ((r ^ m) <= r) & ((m > 0) | (offset <= query))
    bias = jnp.where(seen, 0.0, MASKED).astype(jnp.float32)

    *row1, cache2 = lax.optimization_barrier((*row1, cache2))
    across, beside2 = beside(cache2, 2), beside(cache2, 1)
    state = attend(functools.partial(near_kernel, shape[1]), queries, sel, [*row1, keys0, bias])
    across, *state = lax.optimization_barrier((across, *state))
    row2 = [cache2, beside2, across, beside(across, 1)]
    out = attend(rest_kernel, queries, sel, [*row2, far], state)
    return out.reshape(*shape[:2], LAT)


def solution(mesh):
    placed = (
        P(("groups", "ctx"), None, None),
        P(("groups", "ctx"), None),
        P(("groups", "ctx"), None),
    )
    size = mesh.shape["ctx"]
    shards = shards_rows if size == ROW * DEPTH else shards_general
    return jax.shard_map(
        shards,
        mesh=mesh,
        in_specs=placed,
        out_specs=P(("groups", "ctx"), None, None),
        check_vma=False,
    )
```

```python
import functools
import math

import jax
import jax.numpy as jnp
from jax import lax
from jax.experimental import pallas as pl
from jax.experimental.pallas import tpu as pltpu
from jax.sharding import PartitionSpec as P

LAT = 512
TILE = 64
TOPK = 32
CAP = 1
TILES_DEV = 4
ROW = 4
STAGES = 4
BLOCKS = 4
DEPTH = 4


softmax_scale = 192.0 ** (-0.5)
LOG2E_SCALE = softmax_scale * math.log2(math.e)
MASKED = -1e30


def slot_ranks(holders):
    same = (holders[:, None] == holders[None, :]) & (holders[:, None] >= 0)
    count = holders.shape[0]
    earlier = (
        jnp.arange(count, dtype=jnp.int32)[:, None] < jnp.arange(count, dtype=jnp.int32)[None, :]
    )
    return jnp.sum((same & earlier).astype(jnp.int32), axis=0)


def slot_table(match, ranks, local_tile):
    slots = jnp.arange(CAP, dtype=jnp.int32)
    hits = match[..., None] & (ranks[..., None] == slots)
    return jnp.sum(jnp.where(hits, local_tile[..., None] + 1, 0), axis=-2) - 1


def shards_general(queries, latent_cache, tile_lists):
    width = latent_cache.shape[1]
    listing = tile_lists[0]
    me = lax.axis_index("ctx")
    valid = listing >= 0
    flat_cache = latent_cache.reshape(TILES_DEV, TILE * width)
    peers = lax.axis_size("ctx")
    holders = jnp.where(valid, listing // TILES_DEV, -1)
    ranks = slot_ranks(holders)
    lists_all = lax.all_gather(tile_lists, "ctx", axis=0, tiled=True)
    holders_all = jnp.where(lists_all >= 0, lists_all // TILES_DEV, -1)
    ranks_all = jax.vmap(slot_ranks)(holders_all)
    wanted = slot_table(holders_all == me, ranks_all, lists_all % TILES_DEV)
    outgoing = jnp.take(flat_cache, jnp.clip(wanted, 0, TILES_DEV - 1), axis=0)
    outgoing = jnp.where((wanted >= 0)[..., None], outgoing, jnp.zeros_like(outgoing))
    incoming = lax.all_to_all(outgoing, "ctx", split_axis=0, concat_axis=0, tiled=True)
    incoming = incoming.reshape(peers * CAP, TILE * width)
    position = jnp.clip(holders, 0, peers - 1) * CAP + jnp.clip(ranks, 0, CAP - 1)
    keys = jnp.take(incoming, position, axis=0)
    keys = keys.reshape(TOPK * TILE, width)
    safe = jnp.clip(listing, 0, None)
    offsets = jnp.arange(TILE, dtype=jnp.int32)
    key_pos = (safe[:, None] * TILE + offsets[None, :]).reshape(-1)
    key_ok = jnp.repeat(valid, TILE)
    q_count = queries.shape[0]
    context_dev = TILES_DEV * TILE
    query_pos = me * context_dev + context_dev - q_count + jnp.arange(q_count, dtype=jnp.int32)
    scores = (
        jnp.einsum("qhc,kc->qhk", queries, keys, preferred_element_type=jnp.float32) * softmax_scale
    )
    allowed = (key_ok[None, :] & (key_pos[None, :] <= query_pos[:, None]))[:, None, :]
    scores = jnp.where(allowed, scores, MASKED)
    top = jnp.max(scores, axis=-1, keepdims=True)
    expo = jnp.where(allowed, jnp.exp(scores - top), 0.0)
    total = jnp.sum(expo, axis=-1, keepdims=True)
    weights = expo.astype(jnp.bfloat16)
    summed = jnp.einsum("qhk,kc->qhc", weights, keys[:, :LAT], preferred_element_type=jnp.float32)
    return (summed / total).astype(jnp.bfloat16)


def side_by_side(sel_ref, entry, caches, out_ref):
    for at in range(0, len(caches), 2):
        pair = []
        for upper in (False, True):
            tile = sel_ref[entry + at + upper]
            start = pl.multiple_of(tile // 2 * 2 * TILE, 2 * TILE)
            block = caches[at + upper][:, pl.ds(start, 2 * TILE)]
            swapped = jnp.concatenate([block[:, TILE:], block[:, :TILE]], axis=1)
            pair.append(jnp.where((tile % 2 == 1) != upper, swapped, block))
        out_ref[:, at * TILE : (at + 2) * TILE] = jnp.concatenate(
            [pair[0][:, :TILE], pair[1][:, TILE:]], axis=1
        )


def mixed(factor, without, with_it):
    return without * (1 - factor) + with_it * factor


def lay_out(factors_ref, entry, caches, out_ref):
    for at in range(0, len(caches), 2):
        pair = []
        for one in (at, at + 1):
            row = 2 * (entry + one)
            lower, upper = caches[one][:, : 2 * TILE], caches[one][:, 2 * TILE :]
            block = mixed(factors_ref[row : row + 1, :], lower, upper)
            swapped = jnp.concatenate([block[:, TILE:], block[:, :TILE]], axis=1)
            pair.append(mixed(factors_ref[row + 1 : row + 2, :], block, swapped))
        out_ref[:, at * TILE : (at + 2) * TILE] = jnp.concatenate(
            [pair[0][:, :TILE], pair[1][:, TILE:]], axis=1
        )


def pick_kernel(sel_ref, own_ref, *refs):
    *caches, sent_ref, kept_ref = refs
    side_by_side(sel_ref, 0, caches, sent_ref)
    side_by_side(own_ref, 0, caches, kept_ref)


def pick_tiles(sel, own, caches):
    width = caches[0].shape[0]
    columns = len(caches) * TILE
    vmem = pl.BlockSpec(memory_space=pltpu.VMEM)
    return pl.pallas_call(
        pick_kernel,
        in_specs=[pl.BlockSpec(memory_space=pltpu.SMEM)] * 2 + [vmem] * len(caches),
        out_specs=[vmem] * 2,
        out_shape=[jax.ShapeDtypeStruct((width, columns), caches[0].dtype)] * 2,
        compiler_params=pltpu.CompilerParams(vmem_limit_bytes=6 << 20),
        cost_estimate=pl.CostEstimate(
            flops=0, transcendentals=0, bytes_accessed=8 * columns * width
        ),
        name="pick_tiles",
    )(sel, own, *caches)


def pieces(array):
    return [array[:, at : at + 2 * TILE] for at in range(0, array.shape[1], 2 * TILE)]


def score(queries, keys):
    return jnp.dot(queries, keys, preferred_element_type=jnp.float32)


def weigh(scores, top):
    scaled_top = top * LOG2E_SCALE
    expo = [jnp.exp2(piece * LOG2E_SCALE - scaled_top) for piece in scores]
    total = jnp.sum(functools.reduce(jnp.add, expo), axis=1, keepdims=True)
    expo = jnp.concatenate([piece.astype(jnp.bfloat16) for piece in expo], axis=1)
    return expo, jnp.broadcast_to(total, top.shape)


def tops(scores):
    top = jnp.max(functools.reduce(jnp.maximum, scores), axis=1, keepdims=True)
    return jnp.broadcast_to(top, (top.shape[0], 2 * TILE))


def mix(expo, keys_ref):
    summed = lax.dot_general(
        expo, keys_ref[:LAT, :], (((1,), (1,)), ((), ())), preferred_element_type=jnp.float32
    )
    return pieces(summed)


def near_kernel(heads, factors_ref, *refs):
    caches, refs = refs[:ROW], refs[ROW:]
    own_ref, bias_ref, q_ref, mean_ref, top_ref, total_ref, keys_ref = refs
    half = ROW * TILE
    lay_out(factors_ref, ROW, caches, keys_ref)
    keys_ref[:, half:] = own_ref[...]
    hidden = jnp.where(lax.axis_index("ctx") >= ROW, 0.0, MASKED)
    rows = q_ref.shape[0] // BLOCKS
    for at in range(BLOCKS):
        block = pl.ds(at * rows, rows)
        own = score(q_ref[block, :], own_ref[...])
        bias = bias_ref[pl.ds(at * (rows // heads), rows // heads), :]
        own = own.reshape(rows // heads, heads, -1) + bias[:, None, :]
        scores = [piece + hidden for piece in pieces(score(q_ref[block, :], keys_ref[:, :half]))]
        scores += pieces(own.reshape(rows, -1))
        top = tops(scores)
        expo, total = weigh(scores, top)
        scale = 1.0 / total
        for lane, piece in enumerate(mix(expo, keys_ref)):
            lanes = slice(lane * 2 * TILE, (lane + 1) * 2 * TILE)
            mean_ref[block, lanes] = (piece * scale).astype(mean_ref.dtype)
        top_ref[block, :] = top
        total_ref[block, :] = total


def rest_kernel(factors_ref, *refs):
    caches, refs = refs[:ROW], refs[ROW:]
    far_ref, q_ref, mean_ref, top_ref, total_ref, out_hbm, keys_ref, out_ref, sems = refs
    z = lax.axis_index("ctx") // ROW
    rows = q_ref.shape[0] // BLOCKS

    def put(at):
        block = pl.ds(at * rows, rows)
        return pltpu.make_async_copy(out_ref.at[block, :], out_hbm.at[block, :], sems.at[at])

    @pl.when(z >= DEPTH - 2)
    def _():
        half = ROW * TILE
        lay_out(factors_ref, 2 * ROW, caches, keys_ref)
        keys_ref[:, half:] = far_ref[...]
        hidden = jnp.where(z >= DEPTH - 1, 0.0, MASKED)
        for at in range(BLOCKS):
            block = pl.ds(at * rows, rows)
            far = [piece + hidden for piece in pieces(score(q_ref[block, :], far_ref[...]))]
            scores = pieces(score(q_ref[block, :], keys_ref[:, :half])) + far
            top_before = top_ref[block, :]
            top = jnp.maximum(tops(scores), top_before)
            expo, total = weigh(scores, top)
            before = total_ref[block, :] * jnp.exp2((top_before - top) * LOG2E_SCALE)
            scale = 1.0 / (total + before)
            share = before * scale
            for lane, piece in enumerate(mix(expo, keys_ref)):
                lanes = slice(lane * 2 * TILE, (lane + 1) * 2 * TILE)
                mean = mean_ref[block, lanes].astype(jnp.float32)
                out_ref[block, lanes] = (piece * scale + mean * share).astype(out_ref.dtype)
            put(at).start()

    @pl.when(z < DEPTH - 2)
    def _():
        for at in range(BLOCKS):
            block = pl.ds(at * rows, rows)
            out_ref[block, :] = mean_ref[block, :]
            put(at).start()

    for at in range(BLOCKS):
        put(at).wait()


def attend(kernel, queries, factors, tiles, state=()):
    count, width = queries.shape
    keys = 2 * ROW * TILE
    vmem = pl.BlockSpec(memory_space=pltpu.VMEM)
    near = not state
    scratch = [pltpu.VMEM((width, keys), queries.dtype)]
    if near:
        stats = pltpu.VMEM((count, 2 * TILE), jnp.float32)
        out_shape = [pltpu.VMEM((count, LAT), queries.dtype), stats, stats]
    else:
        out_shape = jax.ShapeDtypeStruct((count, LAT), queries.dtype)
        scratch += [pltpu.VMEM((count, LAT), queries.dtype), pltpu.SemaphoreType.DMA((BLOCKS,))]
    return pl.pallas_call(
        kernel,
        in_specs=[vmem] * (len(tiles) + 2 + len(state)),
        out_specs=[vmem] * 3 if near else pl.BlockSpec(memory_space=pl.ANY),
        out_shape=out_shape,
        scratch_shapes=scratch,
        compiler_params=pltpu.CompilerParams(vmem_limit_bytes=24 << 20),
        cost_estimate=pl.CostEstimate(
            flops=2 * count * keys * (width + LAT),
            transcendentals=count * keys,
            bytes_accessed=2 * count * (width + LAT),
        ),
        name="attend_near" if near else "attend_rest",
    )(factors, *tiles, queries, *state)


def stage_kernel(*refs):
    *refs, sems = refs
    half = len(refs) // 2
    copies = []
    for source_ref, out_ref in zip(refs[:half], refs[half:]):
        rows = source_ref.shape[0] // STAGES
        for at in range(STAGES):
            block = pl.ds(at * rows, rows)
            copies.append(
                pltpu.make_async_copy(
                    source_ref.at[block, :], out_ref.at[block, :], sems.at[len(copies)]
                )
            )
    for copy in copies:
        copy.start()
    for copy in copies:
        copy.wait()


def stage(*arrays):
    return pl.pallas_call(
        stage_kernel,
        in_specs=[pl.BlockSpec(memory_space=pltpu.HBM)] * len(arrays),
        out_specs=[pl.BlockSpec(memory_space=pltpu.VMEM)] * len(arrays),
        out_shape=[pltpu.VMEM(array.shape, array.dtype) for array in arrays],
        scratch_shapes=[pltpu.SemaphoreType.DMA((STAGES * len(arrays),))],
        compiler_params=pltpu.CompilerParams(vmem_limit_bytes=8 << 20),
        cost_estimate=pl.CostEstimate(
            flops=0, transcendentals=0, bytes_accessed=4 * sum(array.size for array in arrays)
        ),
        name="stage",
    )(*(pltpu.with_memory_space_constraint(array, pltpu.HBM) for array in arrays))


def shards_rows(queries, latent_cache, tile_lists):
    size = lax.axis_size("ctx")
    span = size - ROW
    me = lax.axis_index("ctx")
    z, r = me // ROW, me % ROW

    def beside(array, m):
        return lax.ppermute(array, "ctx", [(i, i ^ m) for i in range(size)])

    def further(array, rows, sources):
        return lax.ppermute(array, "ctx", [(i, i + ROW * rows) for i in sources])

    def named_tiles(listing, holders):
        hit = (listing >= 0) & (listing // TILES_DEV == holders[:, None])
        return jnp.sum(jnp.where(hit, listing % TILES_DEV, 0), axis=1)

    shape = queries.shape
    cache = latent_cache.T
    cache1 = further(cache, 1, range(span))
    across = beside(cache, 2)
    far_list = lax.ppermute(tile_lists, "ctx", [(i + span, i) for i in range(ROW)])
    (cache,) = stage(cache)
    cache, across = lax.optimization_barrier((cache, across))
    row0 = [cache, beside(cache, 1), across, beside(across, 1)]

    slot = jnp.arange((DEPTH - 1) * ROW, dtype=jnp.int32)
    sel = named_tiles(tile_lists, ROW * (z - slot // ROW) + (r ^ slot % ROW))

    entry = jnp.arange(2 * (DEPTH - 1) * ROW, dtype=jnp.int32) // 2
    tile = jnp.repeat(sel, 2)
    part = jnp.arange(2 * (DEPTH - 1) * ROW, dtype=jnp.int32) % 2
    factors = jnp.where(part == 0, tile // 2, (tile + entry) % 2).astype(cache.dtype)
    factors = jnp.broadcast_to(factors[:, None], (factors.shape[0], 2 * TILE))

    far_sel = named_tiles(far_list, me ^ jnp.arange(ROW, dtype=jnp.int32))
    far, keys0 = pick_tiles(far_sel, sel, row0)
    cache2 = further(cache1, 1, range(ROW, span))
    across = beside(cache1, 2)
    queries = queries.reshape(-1, shape[2])
    far, queries = lax.optimization_barrier((far, queries))
    (queries,) = stage(queries)
    cache1, queries = lax.optimization_barrier((cache1, queries))
    beside1 = beside(cache1, 1)
    across, far, queries = lax.optimization_barrier((across, far, queries))
    far = further(far, DEPTH - 1, range(ROW))
    row1 = [cache1, beside1, across, beside(across, 1)]

    slot = jnp.arange(ROW * TILE, dtype=jnp.int32)
    m, offset = slot // TILE, slot % TILE
    query = jnp.arange(shape[0], dtype=jnp.int32)[:, None]
    seen = ((r ^ m) <= r) & ((m > 0) | (offset <= query))
    bias = jnp.where(seen, 0.0, MASKED).astype(jnp.float32)

    *row1, cache2 = lax.optimization_barrier((*row1, cache2))
    across, beside2 = beside(cache2, 2), beside(cache2, 1)
    state = attend(functools.partial(near_kernel, shape[1]), queries, factors, [*row1, keys0, bias])
    across, *state = lax.optimization_barrier((across, *state))
    row2 = [cache2, beside2, across, beside(across, 1)]
    out = attend(rest_kernel, queries, factors, [*row2, far], state)
    return out.reshape(*shape[:2], LAT)


def solution(mesh):
    placed = (
        P(("groups", "ctx"), None, None),
        P(("groups", "ctx"), None),
        P(("groups", "ctx"), None),
    )
    size = mesh.shape["ctx"]
    shards = shards_rows if size == ROW * DEPTH else shards_general
    return jax.shard_map(
        shards,
        mesh=mesh,
        in_specs=placed,
        out_specs=P(("groups", "ctx"), None, None),
        check_vma=False,
    )
```

```python
import functools
import math

import jax
import jax.numpy as jnp
from jax import lax
from jax.experimental import pallas as pl
from jax.experimental.pallas import tpu as pltpu
from jax.sharding import PartitionSpec as P

LAT = 512
TILE = 64
TOPK = 32
CAP = 1
TILES_DEV = 4
ROW = 4
STAGES = 4
BLOCKS = 4
DEPTH = 4


softmax_scale = 192.0 ** (-0.5)
LOG2E_SCALE = softmax_scale * math.log2(math.e)
MASKED = -1e30


def slot_ranks(holders):
    same = (holders[:, None] == holders[None, :]) & (holders[:, None] >= 0)
    count = holders.shape[0]
    earlier = (
        jnp.arange(count, dtype=jnp.int32)[:, None] < jnp.arange(count, dtype=jnp.int32)[None, :]
    )
    return jnp.sum((same & earlier).astype(jnp.int32), axis=0)


def slot_table(match, ranks, local_tile):
    slots = jnp.arange(CAP, dtype=jnp.int32)
    hits = match[..., None] & (ranks[..., None] == slots)
    return jnp.sum(jnp.where(hits, local_tile[..., None] + 1, 0), axis=-2) - 1


def shards_general(queries, latent_cache, tile_lists):
    width = latent_cache.shape[1]
    listing = tile_lists[0]
    me = lax.axis_index("ctx")
    valid = listing >= 0
    flat_cache = latent_cache.reshape(TILES_DEV, TILE * width)
    peers = lax.axis_size("ctx")
    holders = jnp.where(valid, listing // TILES_DEV, -1)
    ranks = slot_ranks(holders)
    lists_all = lax.all_gather(tile_lists, "ctx", axis=0, tiled=True)
    holders_all = jnp.where(lists_all >= 0, lists_all // TILES_DEV, -1)
    ranks_all = jax.vmap(slot_ranks)(holders_all)
    wanted = slot_table(holders_all == me, ranks_all, lists_all % TILES_DEV)
    outgoing = jnp.take(flat_cache, jnp.clip(wanted, 0, TILES_DEV - 1), axis=0)
    outgoing = jnp.where((wanted >= 0)[..., None], outgoing, jnp.zeros_like(outgoing))
    incoming = lax.all_to_all(outgoing, "ctx", split_axis=0, concat_axis=0, tiled=True)
    incoming = incoming.reshape(peers * CAP, TILE * width)
    position = jnp.clip(holders, 0, peers - 1) * CAP + jnp.clip(ranks, 0, CAP - 1)
    keys = jnp.take(incoming, position, axis=0)
    keys = keys.reshape(TOPK * TILE, width)
    safe = jnp.clip(listing, 0, None)
    offsets = jnp.arange(TILE, dtype=jnp.int32)
    key_pos = (safe[:, None] * TILE + offsets[None, :]).reshape(-1)
    key_ok = jnp.repeat(valid, TILE)
    q_count = queries.shape[0]
    context_dev = TILES_DEV * TILE
    query_pos = me * context_dev + context_dev - q_count + jnp.arange(q_count, dtype=jnp.int32)
    scores = (
        jnp.einsum("qhc,kc->qhk", queries, keys, preferred_element_type=jnp.float32) * softmax_scale
    )
    allowed = (key_ok[None, :] & (key_pos[None, :] <= query_pos[:, None]))[:, None, :]
    scores = jnp.where(allowed, scores, MASKED)
    top = jnp.max(scores, axis=-1, keepdims=True)
    expo = jnp.where(allowed, jnp.exp(scores - top), 0.0)
    total = jnp.sum(expo, axis=-1, keepdims=True)
    weights = expo.astype(jnp.bfloat16)
    summed = jnp.einsum("qhk,kc->qhc", weights, keys[:, :LAT], preferred_element_type=jnp.float32)
    return (summed / total).astype(jnp.bfloat16)


def side_by_side(sel_ref, entry, caches, out_ref):
    for at in range(0, len(caches), 2):
        pair = []
        for upper in (False, True):
            tile = sel_ref[entry + at + upper]
            start = pl.multiple_of(tile // 2 * 2 * TILE, 2 * TILE)
            block = caches[at + upper][:, pl.ds(start, 2 * TILE)]
            swapped = jnp.concatenate([block[:, TILE:], block[:, :TILE]], axis=1)
            pair.append(jnp.where((tile % 2 == 1) != upper, swapped, block))
        out_ref[:, at * TILE : (at + 2) * TILE] = jnp.concatenate(
            [pair[0][:, :TILE], pair[1][:, TILE:]], axis=1
        )


def mixed(factor, without, with_it):
    return without * (1 - factor) + with_it * factor


def lay_out(factors_ref, entry, caches, out_ref):
    for at in range(0, len(caches), 2):
        pair = []
        for one in (at, at + 1):
            row = 2 * (entry + one)
            lower, upper = caches[one][:, : 2 * TILE], caches[one][:, 2 * TILE :]
            block = mixed(factors_ref[row : row + 1, :], lower, upper)
            swapped = jnp.concatenate([block[:, TILE:], block[:, :TILE]], axis=1)
            pair.append(mixed(factors_ref[row + 1 : row + 2, :], block, swapped))
        out_ref[:, at * TILE : (at + 2) * TILE] = jnp.concatenate(
            [pair[0][:, :TILE], pair[1][:, TILE:]], axis=1
        )


def pick_kernel(sel_ref, own_ref, *refs):
    *caches, sent_ref, kept_ref = refs
    side_by_side(sel_ref, 0, caches, sent_ref)
    side_by_side(own_ref, 0, caches, kept_ref)


def pick_tiles(sel, own, caches):
    width = caches[0].shape[0]
    columns = len(caches) * TILE
    vmem = pl.BlockSpec(memory_space=pltpu.VMEM)
    return pl.pallas_call(
        pick_kernel,
        in_specs=[pl.BlockSpec(memory_space=pltpu.SMEM)] * 2 + [vmem] * len(caches),
        out_specs=[vmem] * 2,
        out_shape=[jax.ShapeDtypeStruct((width, columns), caches[0].dtype)] * 2,
        compiler_params=pltpu.CompilerParams(vmem_limit_bytes=6 << 20),
        cost_estimate=pl.CostEstimate(
            flops=0, transcendentals=0, bytes_accessed=8 * columns * width
        ),
        name="pick_tiles",
    )(sel, own, *caches)


def pieces(array):
    return [array[:, at : at + 2 * TILE] for at in range(0, array.shape[1], 2 * TILE)]


def score(queries, keys):
    return jnp.dot(queries, keys, preferred_element_type=jnp.float32)


def weigh(scores, top):
    scaled_top = top * LOG2E_SCALE
    expo = [jnp.exp2(piece * LOG2E_SCALE - scaled_top) for piece in scores]
    total = jnp.sum(functools.reduce(jnp.add, expo), axis=1, keepdims=True)
    expo = jnp.concatenate([piece.astype(jnp.bfloat16) for piece in expo], axis=1)
    return expo, jnp.broadcast_to(total, top.shape)


def tops(scores):
    top = jnp.max(functools.reduce(jnp.maximum, scores), axis=1, keepdims=True)
    return jnp.broadcast_to(top, (top.shape[0], 2 * TILE))


def mix(expo, keys_ref):
    summed = lax.dot_general(
        expo, keys_ref[:LAT, :], (((1,), (1,)), ((), ())), preferred_element_type=jnp.float32
    )
    return pieces(summed)


def near_kernel(heads, factors_ref, *refs):
    caches, refs = refs[:ROW], refs[ROW:]
    own_ref, bias_ref, q_ref, mean_ref, top_ref, total_ref, keys_ref = refs
    half = ROW * TILE
    lay_out(factors_ref, ROW, caches, keys_ref)
    keys_ref[:, half:] = own_ref[...]
    hidden = jnp.where(lax.axis_index("ctx") >= ROW, 0.0, MASKED)
    rows = q_ref.shape[0] // BLOCKS
    for at in range(BLOCKS):
        block = pl.ds(at * rows, rows)
        own = score(q_ref[block, :], own_ref[...])
        bias = bias_ref[pl.ds(at * (rows // heads), rows // heads), :]
        own = own.reshape(rows // heads, heads, -1) + bias[:, None, :]
        scores = [piece + hidden for piece in pieces(score(q_ref[block, :], keys_ref[:, :half]))]
        scores += pieces(own.reshape(rows, -1))
        top = tops(scores)
        expo, total = weigh(scores, top)
        scale = 1.0 / total
        for lane, piece in enumerate(mix(expo, keys_ref)):
            lanes = slice(lane * 2 * TILE, (lane + 1) * 2 * TILE)
            mean_ref[block, lanes] = (piece * scale).astype(mean_ref.dtype)
        top_ref[block, :] = top
        total_ref[block, :] = total


def rest_kernel(factors_ref, *refs):
    caches, refs = refs[:ROW], refs[ROW:]
    far_ref, q_ref, mean_ref, top_ref, total_ref, out_hbm, keys_ref, out_ref, sems = refs
    z = lax.axis_index("ctx") // ROW
    rows = q_ref.shape[0] // BLOCKS

    def put(at):
        block = pl.ds(at * rows, rows)
        return pltpu.make_async_copy(out_ref.at[block, :], out_hbm.at[block, :], sems.at[at])

    @pl.when(z >= DEPTH - 2)
    def _():
        half = ROW * TILE
        lay_out(factors_ref, 2 * ROW, caches, keys_ref)
        keys_ref[:, half:] = far_ref[...]
        hidden = jnp.where(z >= DEPTH - 1, 0.0, MASKED)
        for at in range(BLOCKS):
            block = pl.ds(at * rows, rows)
            far = [piece + hidden for piece in pieces(score(q_ref[block, :], far_ref[...]))]
            scores = pieces(score(q_ref[block, :], keys_ref[:, :half])) + far
            top_before = top_ref[block, :]
            top = jnp.maximum(tops(scores), top_before)
            expo, total = weigh(scores, top)
            before = total_ref[block, :] * jnp.exp2((top_before - top) * LOG2E_SCALE)
            scale = 1.0 / (total + before)
            share = before * scale
            for lane, piece in enumerate(mix(expo, keys_ref)):
                lanes = slice(lane * 2 * TILE, (lane + 1) * 2 * TILE)
                mean = mean_ref[block, lanes].astype(jnp.float32)
                out_ref[block, lanes] = (piece * scale + mean * share).astype(out_ref.dtype)
            put(at).start()

    @pl.when(z < DEPTH - 2)
    def _():
        for at in range(BLOCKS):
            block = pl.ds(at * rows, rows)
            out_ref[block, :] = mean_ref[block, :]
            put(at).start()

    for at in range(BLOCKS):
        put(at).wait()


def attend(kernel, queries, factors, tiles, state=()):
    count, width = queries.shape
    keys = 2 * ROW * TILE
    vmem = pl.BlockSpec(memory_space=pltpu.VMEM)
    near = not state
    scratch = [pltpu.VMEM((width, keys), queries.dtype)]
    if near:
        stats = pltpu.VMEM((count, 2 * TILE), jnp.float32)
        out_shape = [pltpu.VMEM((count, LAT), queries.dtype), stats, stats]
    else:
        out_shape = jax.ShapeDtypeStruct((count, LAT), queries.dtype)
        scratch += [pltpu.VMEM((count, LAT), queries.dtype), pltpu.SemaphoreType.DMA((BLOCKS,))]
    return pl.pallas_call(
        kernel,
        in_specs=[vmem] * (len(tiles) + 2 + len(state)),
        out_specs=[vmem] * 3 if near else pl.BlockSpec(memory_space=pl.ANY),
        out_shape=out_shape,
        scratch_shapes=scratch,
        compiler_params=pltpu.CompilerParams(vmem_limit_bytes=24 << 20),
        cost_estimate=pl.CostEstimate(
            flops=2 * count * keys * (width + LAT),
            transcendentals=count * keys,
            bytes_accessed=2 * count * (width + LAT),
        ),
        name="attend_near" if near else "attend_rest",
    )(factors, *tiles, queries, *state)


def stage_kernel(*refs):
    *refs, sems = refs
    half = len(refs) // 2
    copies = []
    for source_ref, out_ref in zip(refs[:half], refs[half:]):
        rows = source_ref.shape[0] // STAGES
        for at in range(STAGES):
            block = pl.ds(at * rows, rows)
            copies.append(
                pltpu.make_async_copy(
                    source_ref.at[block, :], out_ref.at[block, :], sems.at[len(copies)]
                )
            )
    for copy in copies:
        copy.start()
    for copy in copies:
        copy.wait()


def stage(*arrays):
    return pl.pallas_call(
        stage_kernel,
        in_specs=[pl.BlockSpec(memory_space=pltpu.HBM)] * len(arrays),
        out_specs=[pl.BlockSpec(memory_space=pltpu.VMEM)] * len(arrays),
        out_shape=[pltpu.VMEM(array.shape, array.dtype) for array in arrays],
        scratch_shapes=[pltpu.SemaphoreType.DMA((STAGES * len(arrays),))],
        compiler_params=pltpu.CompilerParams(vmem_limit_bytes=8 << 20),
        cost_estimate=pl.CostEstimate(
            flops=0, transcendentals=0, bytes_accessed=4 * sum(array.size for array in arrays)
        ),
        name="stage",
    )(*(pltpu.with_memory_space_constraint(array, pltpu.HBM) for array in arrays))


def shards_rows(queries, latent_cache, tile_lists):
    size = lax.axis_size("ctx")
    span = size - ROW
    me = lax.axis_index("ctx")
    z, r = me // ROW, me % ROW

    def beside(array, m):
        return lax.ppermute(array, "ctx", [(i, i ^ m) for i in range(size)])

    def further(array, rows, sources):
        return lax.ppermute(array, "ctx", [(i, i + ROW * rows) for i in sources])

    def named_tiles(listing, holders):
        tile = listing - TILES_DEV * holders[:, None]
        hit = (listing >= 0) & (tile >= 0) & (tile < TILES_DEV)
        return jnp.sum(jnp.where(hit, tile, 0), axis=1)

    shape = queries.shape
    cache = latent_cache.T
    cache1 = further(cache, 1, range(span))
    across = beside(cache, 2)
    far_list = lax.ppermute(tile_lists, "ctx", [(i + span, i) for i in range(ROW)])
    (cache,) = stage(cache)
    cache, across = lax.optimization_barrier((cache, across))
    row0 = [cache, beside(cache, 1), across, beside(across, 1)]

    slot = jnp.arange((DEPTH - 1) * ROW, dtype=jnp.int32)
    sel = named_tiles(tile_lists, ROW * (z - slot // ROW) + (r ^ slot % ROW))

    entry = jnp.arange(2 * (DEPTH - 1) * ROW, dtype=jnp.int32) // 2
    tile = jnp.repeat(sel, 2)
    part = jnp.arange(2 * (DEPTH - 1) * ROW, dtype=jnp.int32) % 2
    factors = jnp.where(part == 0, tile // 2, (tile + entry) % 2).astype(cache.dtype)
    factors = jnp.broadcast_to(factors[:, None], (factors.shape[0], 2 * TILE))

    far_sel = named_tiles(far_list, me ^ jnp.arange(ROW, dtype=jnp.int32))
    far, keys0 = pick_tiles(far_sel, sel, row0)
    cache2 = further(cache1, 1, range(ROW, span))
    across = beside(cache1, 2)
    queries = queries.reshape(-1, shape[2])
    far, queries = lax.optimization_barrier((far, queries))
    (queries,) = stage(queries)
    cache1, queries = lax.optimization_barrier((cache1, queries))
    beside1 = beside(cache1, 1)
    across, far, queries = lax.optimization_barrier((across, far, queries))
    far = further(far, DEPTH - 1, range(ROW))
    row1 = [cache1, beside1, across, beside(across, 1)]

    slot = jnp.arange(ROW * TILE, dtype=jnp.int32)
    m, offset = slot // TILE, slot % TILE
    query = jnp.arange(shape[0], dtype=jnp.int32)[:, None]
    seen = ((r ^ m) <= r) & ((m > 0) | (offset <= query))
    bias = jnp.where(seen, 0.0, MASKED).astype(jnp.float32)

    *row1, cache2 = lax.optimization_barrier((*row1, cache2))
    across, beside2 = beside(cache2, 2), beside(cache2, 1)
    state = attend(functools.partial(near_kernel, shape[1]), queries, factors, [*row1, keys0, bias])
    across, *state = lax.optimization_barrier((across, *state))
    row2 = [cache2, beside2, across, beside(across, 1)]
    out = attend(rest_kernel, queries, factors, [*row2, far], state)
    return out.reshape(*shape[:2], LAT)


def solution(mesh):
    placed = (
        P(("groups", "ctx"), None, None),
        P(("groups", "ctx"), None),
        P(("groups", "ctx"), None),
    )
    size = mesh.shape["ctx"]
    shards = shards_rows if size == ROW * DEPTH else shards_general
    return jax.shard_map(
        shards,
        mesh=mesh,
        in_specs=placed,
        out_specs=P(("groups", "ctx"), None, None),
        check_vma=False,
    )
```

```python
import functools
import math

import jax
import jax.numpy as jnp
from jax import lax
from jax.experimental import pallas as pl
from jax.experimental.pallas import tpu as pltpu
from jax.sharding import PartitionSpec as P

LAT = 512
TILE = 64
TOPK = 32
CAP = 1
TILES_DEV = 4
ROW = 4
STAGES = 4
BLOCKS = 4
DEPTH = 4


softmax_scale = 192.0 ** (-0.5)
LOG2E_SCALE = softmax_scale * math.log2(math.e)
MASKED = -1e30


def slot_ranks(holders):
    same = (holders[:, None] == holders[None, :]) & (holders[:, None] >= 0)
    count = holders.shape[0]
    earlier = (
        jnp.arange(count, dtype=jnp.int32)[:, None] < jnp.arange(count, dtype=jnp.int32)[None, :]
    )
    return jnp.sum((same & earlier).astype(jnp.int32), axis=0)


def slot_table(match, ranks, local_tile):
    slots = jnp.arange(CAP, dtype=jnp.int32)
    hits = match[..., None] & (ranks[..., None] == slots)
    return jnp.sum(jnp.where(hits, local_tile[..., None] + 1, 0), axis=-2) - 1


def shards_general(queries, latent_cache, tile_lists):
    width = latent_cache.shape[1]
    listing = tile_lists[0]
    me = lax.axis_index("ctx")
    valid = listing >= 0
    flat_cache = latent_cache.reshape(TILES_DEV, TILE * width)
    peers = lax.axis_size("ctx")
    holders = jnp.where(valid, listing // TILES_DEV, -1)
    ranks = slot_ranks(holders)
    lists_all = lax.all_gather(tile_lists, "ctx", axis=0, tiled=True)
    holders_all = jnp.where(lists_all >= 0, lists_all // TILES_DEV, -1)
    ranks_all = jax.vmap(slot_ranks)(holders_all)
    wanted = slot_table(holders_all == me, ranks_all, lists_all % TILES_DEV)
    outgoing = jnp.take(flat_cache, jnp.clip(wanted, 0, TILES_DEV - 1), axis=0)
    outgoing = jnp.where((wanted >= 0)[..., None], outgoing, jnp.zeros_like(outgoing))
    incoming = lax.all_to_all(outgoing, "ctx", split_axis=0, concat_axis=0, tiled=True)
    incoming = incoming.reshape(peers * CAP, TILE * width)
    position = jnp.clip(holders, 0, peers - 1) * CAP + jnp.clip(ranks, 0, CAP - 1)
    keys = jnp.take(incoming, position, axis=0)
    keys = keys.reshape(TOPK * TILE, width)
    safe = jnp.clip(listing, 0, None)
    offsets = jnp.arange(TILE, dtype=jnp.int32)
    key_pos = (safe[:, None] * TILE + offsets[None, :]).reshape(-1)
    key_ok = jnp.repeat(valid, TILE)
    q_count = queries.shape[0]
    context_dev = TILES_DEV * TILE
    query_pos = me * context_dev + context_dev - q_count + jnp.arange(q_count, dtype=jnp.int32)
    scores = (
        jnp.einsum("qhc,kc->qhk", queries, keys, preferred_element_type=jnp.float32) * softmax_scale
    )
    allowed = (key_ok[None, :] & (key_pos[None, :] <= query_pos[:, None]))[:, None, :]
    scores = jnp.where(allowed, scores, MASKED)
    top = jnp.max(scores, axis=-1, keepdims=True)
    expo = jnp.where(allowed, jnp.exp(scores - top), 0.0)
    total = jnp.sum(expo, axis=-1, keepdims=True)
    weights = expo.astype(jnp.bfloat16)
    summed = jnp.einsum("qhk,kc->qhc", weights, keys[:, :LAT], preferred_element_type=jnp.float32)
    return (summed / total).astype(jnp.bfloat16)


def side_by_side(sel_ref, entry, caches, out_ref):
    for at in range(0, len(caches), 2):
        pair = []
        for upper in (False, True):
            tile = sel_ref[entry + at + upper]
            start = pl.multiple_of(tile // 2 * 2 * TILE, 2 * TILE)
            block = caches[at + upper][:, pl.ds(start, 2 * TILE)]
            swapped = jnp.concatenate([block[:, TILE:], block[:, :TILE]], axis=1)
            pair.append(jnp.where((tile % 2 == 1) != upper, swapped, block))
        out_ref[:, at * TILE : (at + 2) * TILE] = jnp.concatenate(
            [pair[0][:, :TILE], pair[1][:, TILE:]], axis=1
        )


def mixed(factor, without, with_it):
    return without * (1 - factor) + with_it * factor


def lay_out(factors_ref, entry, caches, out_ref):
    for at in range(0, len(caches), 2):
        pair = []
        for one in (at, at + 1):
            row = 2 * (entry + one)
            lower, upper = caches[one][:, : 2 * TILE], caches[one][:, 2 * TILE :]
            block = mixed(factors_ref[row : row + 1, :], lower, upper)
            swapped = jnp.concatenate([block[:, TILE:], block[:, :TILE]], axis=1)
            pair.append(mixed(factors_ref[row + 1 : row + 2, :], block, swapped))
        out_ref[:, at * TILE : (at + 2) * TILE] = jnp.concatenate(
            [pair[0][:, :TILE], pair[1][:, TILE:]], axis=1
        )


def pick_kernel(sel_ref, own_ref, *refs):
    *caches, sent_ref, kept_ref = refs
    side_by_side(sel_ref, 0, caches, sent_ref)
    side_by_side(own_ref, 0, caches, kept_ref)


def pick_tiles(sel, own, caches):
    width = caches[0].shape[0]
    columns = len(caches) * TILE
    vmem = pl.BlockSpec(memory_space=pltpu.VMEM)
    return pl.pallas_call(
        pick_kernel,
        in_specs=[pl.BlockSpec(memory_space=pltpu.SMEM)] * 2 + [vmem] * len(caches),
        out_specs=[vmem] * 2,
        out_shape=[jax.ShapeDtypeStruct((width, columns), caches[0].dtype)] * 2,
        compiler_params=pltpu.CompilerParams(vmem_limit_bytes=6 << 20),
        cost_estimate=pl.CostEstimate(
            flops=0, transcendentals=0, bytes_accessed=8 * columns * width
        ),
        name="pick_tiles",
    )(sel, own, *caches)


def pieces(array):
    return [array[:, at : at + 2 * TILE] for at in range(0, array.shape[1], 2 * TILE)]


def score(queries, keys):
    return jnp.dot(queries, keys, preferred_element_type=jnp.float32)


def weigh(scores, top):
    scaled_top = top * LOG2E_SCALE
    expo = [jnp.exp2(piece * LOG2E_SCALE - scaled_top) for piece in scores]
    total = jnp.sum(functools.reduce(jnp.add, expo), axis=1, keepdims=True)
    expo = jnp.concatenate([piece.astype(jnp.bfloat16) for piece in expo], axis=1)
    return expo, jnp.broadcast_to(total, top.shape)


def tops(scores):
    top = jnp.max(functools.reduce(jnp.maximum, scores), axis=1, keepdims=True)
    return jnp.broadcast_to(top, (top.shape[0], 2 * TILE))


def mix(expo, keys_ref):
    summed = lax.dot_general(
        expo, keys_ref[:LAT, :], (((1,), (1,)), ((), ())), preferred_element_type=jnp.float32
    )
    return pieces(summed)


def near_kernel(heads, factors_ref, *refs):
    caches, refs = refs[:ROW], refs[ROW:]
    own_ref, bias_ref, q_ref, mean_ref, top_ref, total_ref, keys_ref = refs
    half = ROW * TILE
    lay_out(factors_ref, ROW, caches, keys_ref)
    keys_ref[:, half:] = own_ref[...]
    hidden = jnp.where(lax.axis_index("ctx") >= ROW, 0.0, MASKED)
    rows = q_ref.shape[0] // BLOCKS
    for at in range(BLOCKS):
        block = pl.ds(at * rows, rows)
        own = score(q_ref[block, :], own_ref[...])
        bias = bias_ref[pl.ds(at * (rows // heads), rows // heads), :]
        own = own.reshape(rows // heads, heads, -1) + bias[:, None, :]
        scores = [piece + hidden for piece in pieces(score(q_ref[block, :], keys_ref[:, :half]))]
        scores += pieces(own.reshape(rows, -1))
        top = tops(scores)
        expo, total = weigh(scores, top)
        scale = 1.0 / total
        for lane, piece in enumerate(mix(expo, keys_ref)):
            lanes = slice(lane * 2 * TILE, (lane + 1) * 2 * TILE)
            mean_ref[block, lanes] = (piece * scale).astype(mean_ref.dtype)
        top_ref[block, :] = top
        total_ref[block, :] = total


def rest_kernel(factors_ref, *refs):
    caches, refs = refs[:ROW], refs[ROW:]
    far_ref, q_ref, mean_ref, top_ref, total_ref, out_hbm, keys_ref, out_ref, sems = refs
    z = lax.axis_index("ctx") // ROW
    rows = q_ref.shape[0] // BLOCKS

    def put(at):
        block = pl.ds(at * rows, rows)
        return pltpu.make_async_copy(out_ref.at[block, :], out_hbm.at[block, :], sems.at[at])

    @pl.when(z >= DEPTH - 2)
    def _():
        half = ROW * TILE
        lay_out(factors_ref, 2 * ROW, caches, keys_ref)
        keys_ref[:, half:] = far_ref[...]
        hidden = jnp.where(z >= DEPTH - 1, 0.0, MASKED)
        for at in range(BLOCKS):
            block = pl.ds(at * rows, rows)
            far = [piece + hidden for piece in pieces(score(q_ref[block, :], far_ref[...]))]
            scores = pieces(score(q_ref[block, :], keys_ref[:, :half])) + far
            top_before = top_ref[block, :]
            top = jnp.maximum(tops(scores), top_before)
            expo, total = weigh(scores, top)
            before = total_ref[block, :] * jnp.exp2((top_before - top) * LOG2E_SCALE)
            scale = 1.0 / (total + before)
            share = before * scale
            for lane, piece in enumerate(mix(expo, keys_ref)):
                lanes = slice(lane * 2 * TILE, (lane + 1) * 2 * TILE)
                mean = mean_ref[block, lanes].astype(jnp.float32)
                out_ref[block, lanes] = (piece * scale + mean * share).astype(out_ref.dtype)
            put(at).start()

    @pl.when(z < DEPTH - 2)
    def _():
        for at in range(BLOCKS):
            block = pl.ds(at * rows, rows)
            out_ref[block, :] = mean_ref[block, :]
            put(at).start()

    for at in range(BLOCKS):
        put(at).wait()


def attend(kernel, queries, factors, tiles, state=()):
    count, width = queries.shape
    keys = 2 * ROW * TILE
    vmem = pl.BlockSpec(memory_space=pltpu.VMEM)
    near = not state
    scratch = [pltpu.VMEM((width, keys), queries.dtype)]
    if near:
        stats = pltpu.VMEM((count, 2 * TILE), jnp.float32)
        out_shape = [pltpu.VMEM((count, LAT), queries.dtype), stats, stats]
    else:
        out_shape = jax.ShapeDtypeStruct((count, LAT), queries.dtype)
        scratch += [pltpu.VMEM((count, LAT), queries.dtype), pltpu.SemaphoreType.DMA((BLOCKS,))]
    return pl.pallas_call(
        kernel,
        in_specs=[vmem] * (len(tiles) + 2 + len(state)),
        out_specs=[vmem] * 3 if near else pl.BlockSpec(memory_space=pl.ANY),
        out_shape=out_shape,
        scratch_shapes=scratch,
        compiler_params=pltpu.CompilerParams(vmem_limit_bytes=24 << 20),
        cost_estimate=pl.CostEstimate(
            flops=2 * count * keys * (width + LAT),
            transcendentals=count * keys,
            bytes_accessed=2 * count * (width + LAT),
        ),
        name="attend_near" if near else "attend_rest",
    )(factors, *tiles, queries, *state)


def stage_kernel(*refs):
    *refs, sems = refs
    half = len(refs) // 2
    copies = []
    for source_ref, out_ref in zip(refs[:half], refs[half:]):
        rows = source_ref.shape[0] // STAGES
        for at in range(STAGES):
            block = pl.ds(at * rows, rows)
            copies.append(
                pltpu.make_async_copy(
                    source_ref.at[block, :], out_ref.at[block, :], sems.at[len(copies)]
                )
            )
    for copy in copies:
        copy.start()
    for copy in copies:
        copy.wait()


def stage(*arrays):
    return pl.pallas_call(
        stage_kernel,
        in_specs=[pl.BlockSpec(memory_space=pltpu.HBM)] * len(arrays),
        out_specs=[pl.BlockSpec(memory_space=pltpu.VMEM)] * len(arrays),
        out_shape=[pltpu.VMEM(array.shape, array.dtype) for array in arrays],
        scratch_shapes=[pltpu.SemaphoreType.DMA((STAGES * len(arrays),))],
        compiler_params=pltpu.CompilerParams(vmem_limit_bytes=8 << 20),
        cost_estimate=pl.CostEstimate(
            flops=0, transcendentals=0, bytes_accessed=4 * sum(array.size for array in arrays)
        ),
        name="stage",
    )(*(pltpu.with_memory_space_constraint(array, pltpu.HBM) for array in arrays))


def shards_rows(queries, latent_cache, tile_lists):
    size = lax.axis_size("ctx")
    span = size - ROW
    me = lax.axis_index("ctx")
    z, r = me // ROW, me % ROW

    def beside(array, m):
        return lax.ppermute(array, "ctx", [(i, i ^ m) for i in range(size)])

    def further(array, rows, sources):
        return lax.ppermute(array, "ctx", [(i, i + ROW * rows) for i in sources])

    def named_tiles(listing, holders):
        tile = listing - TILES_DEV * holders[:, None]
        hit = (listing >= 0) & (tile >= 0) & (tile < TILES_DEV)
        return jnp.sum(jnp.where(hit, tile, 0), axis=1)

    shape = queries.shape
    cache = latent_cache.T
    cache1 = further(cache, 1, range(span))
    across = beside(cache, 2)
    far_list = lax.ppermute(tile_lists, "ctx", [(i + span, i) for i in range(ROW)])
    (cache,) = stage(cache)
    cache, across = lax.optimization_barrier((cache, across))
    row0 = [cache, beside(cache, 1), across, beside(across, 1)]

    slot = jnp.arange((DEPTH - 1) * ROW, dtype=jnp.int32)
    sel = named_tiles(tile_lists, ROW * (z - slot // ROW) + (r ^ slot % ROW))

    entry = jnp.arange(2 * (DEPTH - 1) * ROW, dtype=jnp.int32) // 2
    tile = jnp.repeat(sel, 2)
    part = jnp.arange(2 * (DEPTH - 1) * ROW, dtype=jnp.int32) % 2
    factors = jnp.where(part == 0, tile // 2, (tile + entry) % 2).astype(cache.dtype)
    factors = jnp.broadcast_to(factors[:, None], (factors.shape[0], 2 * TILE))

    far_sel = named_tiles(far_list, me ^ jnp.arange(ROW, dtype=jnp.int32))
    far, keys0 = pick_tiles(far_sel, sel, row0)
    cache2 = further(cache1, 1, range(ROW, span))
    across = beside(cache1, 2)
    queries = queries.reshape(-1, shape[2])
    far, queries = lax.optimization_barrier((far, queries))
    (queries,) = stage(queries)
    cache1, queries = lax.optimization_barrier((cache1, queries))
    beside1 = beside(cache1, 1)
    across, far, queries = lax.optimization_barrier((across, far, queries))
    far = further(far, DEPTH - 1, range(ROW))
    row1 = [cache1, beside1, across, beside(across, 1)]

    slot = jnp.arange(ROW * TILE, dtype=jnp.int32)
    m, offset = slot // TILE, slot % TILE
    query = jnp.arange(shape[0], dtype=jnp.int32)[:, None]
    seen = ((r ^ m) <= r) & ((m > 0) | (offset <= query))
    bias = jnp.where(seen, 0.0, MASKED).astype(jnp.float32)

    *row1, cache2 = lax.optimization_barrier((*row1, cache2))
    across = beside(cache2, 2)
    state = attend(functools.partial(near_kernel, shape[1]), queries, factors, [*row1, keys0, bias])
    cache2, *state = lax.optimization_barrier((cache2, *state))
    beside2 = beside(cache2, 1)
    across, *state = lax.optimization_barrier((across, *state))
    row2 = [cache2, beside2, across, beside(across, 1)]
    out = attend(rest_kernel, queries, factors, [*row2, far], state)
    return out.reshape(*shape[:2], LAT)


def solution(mesh):
    placed = (
        P(("groups", "ctx"), None, None),
        P(("groups", "ctx"), None),
        P(("groups", "ctx"), None),
    )
    size = mesh.shape["ctx"]
    shards = shards_rows if size == ROW * DEPTH else shards_general
    return jax.shard_map(
        shards,
        mesh=mesh,
        in_specs=placed,
        out_specs=P(("groups", "ctx"), None, None),
        check_vma=False,
    )
```

```python
import functools
import math

import jax
import jax.numpy as jnp
from jax import lax
from jax.experimental import pallas as pl
from jax.experimental.pallas import tpu as pltpu
from jax.sharding import PartitionSpec as P

LAT = 512
TILE = 64
TOPK = 32
CAP = 1
TILES_DEV = 4
ROW = 4
STAGES = 4
BLOCKS = 4
DEPTH = 4


softmax_scale = 192.0 ** (-0.5)
LOG2E_SCALE = softmax_scale * math.log2(math.e)
MASKED = -1e30


def slot_ranks(holders):
    same = (holders[:, None] == holders[None, :]) & (holders[:, None] >= 0)
    count = holders.shape[0]
    earlier = (
        jnp.arange(count, dtype=jnp.int32)[:, None] < jnp.arange(count, dtype=jnp.int32)[None, :]
    )
    return jnp.sum((same & earlier).astype(jnp.int32), axis=0)


def slot_table(match, ranks, local_tile):
    slots = jnp.arange(CAP, dtype=jnp.int32)
    hits = match[..., None] & (ranks[..., None] == slots)
    return jnp.sum(jnp.where(hits, local_tile[..., None] + 1, 0), axis=-2) - 1


def shards_general(queries, latent_cache, tile_lists):
    width = latent_cache.shape[1]
    listing = tile_lists[0]
    me = lax.axis_index("ctx")
    valid = listing >= 0
    flat_cache = latent_cache.reshape(TILES_DEV, TILE * width)
    peers = lax.axis_size("ctx")
    holders = jnp.where(valid, listing // TILES_DEV, -1)
    ranks = slot_ranks(holders)
    lists_all = lax.all_gather(tile_lists, "ctx", axis=0, tiled=True)
    holders_all = jnp.where(lists_all >= 0, lists_all // TILES_DEV, -1)
    ranks_all = jax.vmap(slot_ranks)(holders_all)
    wanted = slot_table(holders_all == me, ranks_all, lists_all % TILES_DEV)
    outgoing = jnp.take(flat_cache, jnp.clip(wanted, 0, TILES_DEV - 1), axis=0)
    outgoing = jnp.where((wanted >= 0)[..., None], outgoing, jnp.zeros_like(outgoing))
    incoming = lax.all_to_all(outgoing, "ctx", split_axis=0, concat_axis=0, tiled=True)
    incoming = incoming.reshape(peers * CAP, TILE * width)
    position = jnp.clip(holders, 0, peers - 1) * CAP + jnp.clip(ranks, 0, CAP - 1)
    keys = jnp.take(incoming, position, axis=0)
    keys = keys.reshape(TOPK * TILE, width)
    safe = jnp.clip(listing, 0, None)
    offsets = jnp.arange(TILE, dtype=jnp.int32)
    key_pos = (safe[:, None] * TILE + offsets[None, :]).reshape(-1)
    key_ok = jnp.repeat(valid, TILE)
    q_count = queries.shape[0]
    context_dev = TILES_DEV * TILE
    query_pos = me * context_dev + context_dev - q_count + jnp.arange(q_count, dtype=jnp.int32)
    scores = (
        jnp.einsum("qhc,kc->qhk", queries, keys, preferred_element_type=jnp.float32) * softmax_scale
    )
    allowed = (key_ok[None, :] & (key_pos[None, :] <= query_pos[:, None]))[:, None, :]
    scores = jnp.where(allowed, scores, MASKED)
    top = jnp.max(scores, axis=-1, keepdims=True)
    expo = jnp.where(allowed, jnp.exp(scores - top), 0.0)
    total = jnp.sum(expo, axis=-1, keepdims=True)
    weights = expo.astype(jnp.bfloat16)
    summed = jnp.einsum("qhk,kc->qhc", weights, keys[:, :LAT], preferred_element_type=jnp.float32)
    return (summed / total).astype(jnp.bfloat16)


def side_by_side(sel_ref, entry, caches, out_ref):
    for at in range(0, len(caches), 2):
        pair = []
        for upper in (False, True):
            tile = sel_ref[entry + at + upper]
            start = pl.multiple_of(tile // 2 * 2 * TILE, 2 * TILE)
            block = caches[at + upper][:, pl.ds(start, 2 * TILE)]
            swapped = jnp.concatenate([block[:, TILE:], block[:, :TILE]], axis=1)
            pair.append(jnp.where((tile % 2 == 1) != upper, swapped, block))
        out_ref[:, at * TILE : (at + 2) * TILE] = jnp.concatenate(
            [pair[0][:, :TILE], pair[1][:, TILE:]], axis=1
        )


def mixed(factor, without, with_it):
    return without * (1 - factor) + with_it * factor


def lay_out(factors_ref, entry, caches, out_ref):
    for at in range(0, len(caches), 2):
        pair = []
        for one in (at, at + 1):
            row = 2 * (entry + one)
            lower, upper = caches[one][:, : 2 * TILE], caches[one][:, 2 * TILE :]
            block = mixed(factors_ref[row : row + 1, :], lower, upper)
            swapped = jnp.concatenate([block[:, TILE:], block[:, :TILE]], axis=1)
            pair.append(mixed(factors_ref[row + 1 : row + 2, :], block, swapped))
        out_ref[:, at * TILE : (at + 2) * TILE] = jnp.concatenate(
            [pair[0][:, :TILE], pair[1][:, TILE:]], axis=1
        )


def pick_kernel(sel_ref, own_ref, *refs):
    *caches, sent_ref, kept_ref = refs
    side_by_side(sel_ref, 0, caches, sent_ref)
    side_by_side(own_ref, 0, caches, kept_ref)


def pick_tiles(sel, own, caches):
    width = caches[0].shape[0]
    columns = len(caches) * TILE
    vmem = pl.BlockSpec(memory_space=pltpu.VMEM)
    return pl.pallas_call(
        pick_kernel,
        in_specs=[pl.BlockSpec(memory_space=pltpu.SMEM)] * 2 + [vmem] * len(caches),
        out_specs=[vmem] * 2,
        out_shape=[jax.ShapeDtypeStruct((width, columns), caches[0].dtype)] * 2,
        compiler_params=pltpu.CompilerParams(vmem_limit_bytes=6 << 20),
        cost_estimate=pl.CostEstimate(
            flops=0, transcendentals=0, bytes_accessed=8 * columns * width
        ),
        name="pick_tiles",
    )(sel, own, *caches)


def pieces(array):
    return [array[:, at : at + 2 * TILE] for at in range(0, array.shape[1], 2 * TILE)]


def score(queries, keys):
    return jnp.dot(queries, keys, preferred_element_type=jnp.float32)


def weigh(scores, top):
    scaled_top = top * LOG2E_SCALE
    expo = [jnp.exp2(piece * LOG2E_SCALE - scaled_top) for piece in scores]
    total = jnp.sum(functools.reduce(jnp.add, expo), axis=1, keepdims=True)
    expo = jnp.concatenate([piece.astype(jnp.bfloat16) for piece in expo], axis=1)
    return expo, jnp.broadcast_to(total, top.shape)


def tops(scores):
    top = jnp.max(functools.reduce(jnp.maximum, scores), axis=1, keepdims=True)
    return jnp.broadcast_to(top, (top.shape[0], 2 * TILE))


def mix(expo, keys_ref):
    summed = lax.dot_general(
        expo, keys_ref[:LAT, :], (((1,), (1,)), ((), ())), preferred_element_type=jnp.float32
    )
    return pieces(summed)


def near_kernel(heads, factors_ref, *refs):
    caches, refs = refs[:ROW], refs[ROW:]
    own_ref, bias_ref, q_ref, mean_ref, top_ref, total_ref, keys_ref = refs
    half = ROW * TILE
    lay_out(factors_ref, ROW, caches, keys_ref)
    keys_ref[:, half:] = own_ref[...]
    hidden = jnp.where(lax.axis_index("ctx") >= ROW, 0.0, MASKED)
    rows = q_ref.shape[0] // BLOCKS
    for at in range(BLOCKS):
        block = pl.ds(at * rows, rows)
        own = score(q_ref[block, :], own_ref[...])
        bias = bias_ref[pl.ds(at * (rows // heads), rows // heads), :]
        own = own.reshape(rows // heads, heads, -1) + bias[:, None, :]
        scores = [piece + hidden for piece in pieces(score(q_ref[block, :], keys_ref[:, :half]))]
        scores += pieces(own.reshape(rows, -1))
        top = tops(scores)
        expo, total = weigh(scores, top)
        scale = 1.0 / total
        for lane, piece in enumerate(mix(expo, keys_ref)):
            lanes = slice(lane * 2 * TILE, (lane + 1) * 2 * TILE)
            mean_ref[block, lanes] = (piece * scale).astype(mean_ref.dtype)
        top_ref[block, :] = top
        total_ref[block, :] = total


def rest_kernel(factors_ref, *refs):
    caches, refs = refs[:ROW], refs[ROW:]
    far_ref, q_ref, mean_ref, top_ref, total_ref, out_hbm, keys_ref, out_ref, sems = refs
    z = lax.axis_index("ctx") // ROW
    rows = q_ref.shape[0] // BLOCKS

    def put(at):
        block = pl.ds(at * rows, rows)
        return pltpu.make_async_copy(out_ref.at[block, :], out_hbm.at[block, :], sems.at[at])

    @pl.when(z >= DEPTH - 2)
    def _():
        half = ROW * TILE
        lay_out(factors_ref, 2 * ROW, caches, keys_ref)
        keys_ref[:, half:] = far_ref[...]
        hidden = jnp.where(z >= DEPTH - 1, 0.0, MASKED)
        for at in range(BLOCKS):
            block = pl.ds(at * rows, rows)
            far = [piece + hidden for piece in pieces(score(q_ref[block, :], far_ref[...]))]
            scores = pieces(score(q_ref[block, :], keys_ref[:, :half])) + far
            top_before = top_ref[block, :]
            top = jnp.maximum(tops(scores), top_before)
            expo, total = weigh(scores, top)
            before = total_ref[block, :] * jnp.exp2((top_before - top) * LOG2E_SCALE)
            scale = 1.0 / (total + before)
            share = before * scale
            for lane, piece in enumerate(mix(expo, keys_ref)):
                lanes = slice(lane * 2 * TILE, (lane + 1) * 2 * TILE)
                mean = mean_ref[block, lanes].astype(jnp.float32)
                out_ref[block, lanes] = (piece * scale + mean * share).astype(out_ref.dtype)
            put(at).start()

    @pl.when(z < DEPTH - 2)
    def _():
        for at in range(BLOCKS):
            block = pl.ds(at * rows, rows)
            out_ref[block, :] = mean_ref[block, :]
            put(at).start()

    for at in range(BLOCKS):
        put(at).wait()


def attend(kernel, queries, factors, tiles, state=()):
    count, width = queries.shape
    keys = 2 * ROW * TILE
    vmem = pl.BlockSpec(memory_space=pltpu.VMEM)
    near = not state
    scratch = [pltpu.VMEM((width, keys), queries.dtype)]
    if near:
        stats = pltpu.VMEM((count, 2 * TILE), jnp.float32)
        out_shape = [pltpu.VMEM((count, LAT), queries.dtype), stats, stats]
    else:
        out_shape = jax.ShapeDtypeStruct((count, LAT), queries.dtype)
        scratch += [pltpu.VMEM((count, LAT), queries.dtype), pltpu.SemaphoreType.DMA((BLOCKS,))]
    return pl.pallas_call(
        kernel,
        in_specs=[vmem] * (len(tiles) + 2 + len(state)),
        out_specs=[vmem] * 3 if near else pl.BlockSpec(memory_space=pl.ANY),
        out_shape=out_shape,
        scratch_shapes=scratch,
        compiler_params=pltpu.CompilerParams(vmem_limit_bytes=24 << 20),
        cost_estimate=pl.CostEstimate(
            flops=2 * count * keys * (width + LAT),
            transcendentals=count * keys,
            bytes_accessed=2 * count * (width + LAT),
        ),
        name="attend_near" if near else "attend_rest",
    )(factors, *tiles, queries, *state)


def stage_kernel(*refs):
    *refs, sems = refs
    half = len(refs) // 2
    copies = []
    for source_ref, out_ref in zip(refs[:half], refs[half:]):
        rows = source_ref.shape[0] // STAGES
        for at in range(STAGES):
            block = pl.ds(at * rows, rows)
            copies.append(
                pltpu.make_async_copy(
                    source_ref.at[block, :], out_ref.at[block, :], sems.at[len(copies)]
                )
            )
    for copy in copies:
        copy.start()
    for copy in copies:
        copy.wait()


def stage(*arrays):
    return pl.pallas_call(
        stage_kernel,
        in_specs=[pl.BlockSpec(memory_space=pltpu.HBM)] * len(arrays),
        out_specs=[pl.BlockSpec(memory_space=pltpu.VMEM)] * len(arrays),
        out_shape=[pltpu.VMEM(array.shape, array.dtype) for array in arrays],
        scratch_shapes=[pltpu.SemaphoreType.DMA((STAGES * len(arrays),))],
        compiler_params=pltpu.CompilerParams(vmem_limit_bytes=8 << 20),
        cost_estimate=pl.CostEstimate(
            flops=0, transcendentals=0, bytes_accessed=4 * sum(array.size for array in arrays)
        ),
        name="stage",
    )(*(pltpu.with_memory_space_constraint(array, pltpu.HBM) for array in arrays))


def shards_rows(queries, latent_cache, tile_lists):
    size = lax.axis_size("ctx")
    span = size - ROW
    me = lax.axis_index("ctx")
    z, r = me // ROW, me % ROW

    def beside(array, m):
        return lax.ppermute(array, "ctx", [(i, i ^ m) for i in range(size)])

    def further(array, rows, sources):
        return lax.ppermute(array, "ctx", [(i, i + ROW * rows) for i in sources])

    def named_tiles(listing, holders):
        tile = listing - TILES_DEV * holders[:, None]
        hit = (listing >= 0) & (tile >= 0) & (tile < TILES_DEV)
        return jnp.sum(jnp.where(hit, tile, 0), axis=1)

    shape = queries.shape
    cache = latent_cache.T
    cache1 = further(cache, 1, range(span))
    across = beside(cache, 2)
    far_list = lax.ppermute(tile_lists, "ctx", [(i + span, i) for i in range(ROW)])
    (cache,) = stage(cache)
    cache, across = lax.optimization_barrier((cache, across))
    row0 = [cache, beside(cache, 1), across, beside(across, 1)]

    slot = jnp.arange((DEPTH - 1) * ROW, dtype=jnp.int32)
    sel = named_tiles(tile_lists, ROW * (z - slot // ROW) + (r ^ slot % ROW))

    entry = jnp.arange(2 * (DEPTH - 1) * ROW, dtype=jnp.int32) // 2
    tile = jnp.repeat(sel, 2)
    part = jnp.arange(2 * (DEPTH - 1) * ROW, dtype=jnp.int32) % 2
    factors = jnp.where(part == 0, tile // 2, (tile + entry) % 2).astype(cache.dtype)
    factors = jnp.broadcast_to(factors[:, None], (factors.shape[0], 2 * TILE))

    far_sel = named_tiles(far_list, me ^ jnp.arange(ROW, dtype=jnp.int32))
    far, keys0 = pick_tiles(far_sel, sel, row0)
    cache2 = further(cache1, 1, range(ROW, span))
    across = beside(cache1, 2)
    queries = queries.reshape(-1, shape[2])
    far, queries = lax.optimization_barrier((far, queries))
    beside1 = beside(cache1, 1)
    (queries,) = stage(queries)
    across, far, queries = lax.optimization_barrier((across, far, queries))
    far = further(far, DEPTH - 1, range(ROW))
    row1 = [cache1, beside1, across, beside(across, 1)]

    slot = jnp.arange(ROW * TILE, dtype=jnp.int32)
    m, offset = slot // TILE, slot % TILE
    query = jnp.arange(shape[0], dtype=jnp.int32)[:, None]
    seen = ((r ^ m) <= r) & ((m > 0) | (offset <= query))
    bias = jnp.where(seen, 0.0, MASKED).astype(jnp.float32)

    *row1, cache2 = lax.optimization_barrier((*row1, cache2))
    across, beside2 = beside(cache2, 2), beside(cache2, 1)
    state = attend(functools.partial(near_kernel, shape[1]), queries, factors, [*row1, keys0, bias])
    across, *state = lax.optimization_barrier((across, *state))
    row2 = [cache2, beside2, across, beside(across, 1)]
    out = attend(rest_kernel, queries, factors, [*row2, far], state)
    return out.reshape(*shape[:2], LAT)


def solution(mesh):
    placed = (
        P(("groups", "ctx"), None, None),
        P(("groups", "ctx"), None),
        P(("groups", "ctx"), None),
    )
    size = mesh.shape["ctx"]
    shards = shards_rows if size == ROW * DEPTH else shards_general
    return jax.shard_map(
        shards,
        mesh=mesh,
        in_specs=placed,
        out_specs=P(("groups", "ctx"), None, None),
        check_vma=False,
    )
```
